32 devices in a mesh: island: 4 (over y, core), fsdp: 8 (over z, x).
Axes of the slice: x: 2, y: 2, z: 4, core: 2. Of those that a mesh axis runs over, the one named last changes fastest.
Arguments:
- tokens: bfloat16 [4, 2048, 8192], P('island', 'fsdp'), may hold values from -6 to 6
- cotangent: bfloat16 [4, 2048, 512], P('island', 'fsdp'), may hold values from -6 to 6
- key_weight: bfloat16 [4, 8192, 512], P('island', 'fsdp'), may hold values from -0.0625 to 0.0625
- quant_codes: int32 [4, 128, 8192], P('island', 'fsdp'), may hold values from 0 to 15
- zero_points: int32 [4, 128, 64], P('island', 'fsdp'), may hold values from 0 to 15
- minima: float32 [4, 128, 64], P('island', 'fsdp'), may hold values from -0.5 to 0.5
- quant_steps: float32 [4, 128, 64], P('island', 'fsdp'), may hold values from 0.01 to 0.1
- momentum: float32 [128, 8192], P('fsdp'), may hold values from -4 to 4
- params: float32 [128, 8192], P('fsdp'), may hold values from -6 to 6
Outputs:
- projected: bfloat16 [4, 2048, 512], P('island', 'fsdp')
- token_grad: bfloat16 [4, 2048, 8192], P('island', 'fsdp')
- weight_grad: float32 [4, 8192, 512], P('island', 'fsdp')
- new_momentum: float32 [128, 8192], P('fsdp')
- new_params: float32 [128, 8192], P('fsdp')
The draws below stay inside these ranges and needn't reach their ends.
All inputs are finite; a program needn't handle non-finite values.
Results may differ from the reference program's by a relative error of at most 0.0054.
Values may be sent and summed in bfloat16 or wider, within the bound.
A program may use at most 128 MiB of HBM per device.

```python
import math
import jax
import jax.numpy as jnp
from jax import lax

D = 8192
HEAD = 128
KV_HEADS = 4
GROUP = 128
ISLAND_TOK = 2048
FRAG = 128
GROUPS = 64
N_ISLAND = 4


def place_ends(entries, key, low, top_value):
    spot = [jax.random.randint(jax.random.fold_in(key, axis), (), 0, length) for axis, length in enumerate(entries.shape)]
    main_axis = entries.shape.index(max(entries.shape))
    next_to = spot[:main_axis] + [(spot[main_axis] + 1) % entries.shape[main_axis]] + spot[main_axis + 1:]
    return entries.at[tuple(spot)].set(low).at[tuple(next_to)].set(top_value)


def levels(stream_key, dims, shards, smallest, high):
    loudness, own = 1.0, jax.random.fold_in(stream_key, 6)
    for axis_at, shards_of in shards:
        heights = jnp.exp(jax.random.uniform(jax.random.fold_in(own, axis_at), (shards_of,), jnp.float32, smallest / len(shards), high / len(shards)))
        loudness = loudness * jnp.repeat(heights, dims[axis_at] // shards_of).reshape([-1 if axis == axis_at else 1 for axis in range(len(dims))])
    return loudness


def normal_values(key, extent, scale, most, pieces=(), dtype=jnp.bfloat16):
    gain = levels(key, extent, pieces, -0.22, 0.18) if pieces else 1.0
    array = jax.random.normal(key, extent, jnp.float32) * scale * gain
    return jnp.minimum(jnp.maximum(array, -most), most).astype(dtype)


def setup_inputs(seed: int = 0) -> dict:
    seeds = jax.random.split(jax.random.key(seed), 10)
    tokens = normal_values(seeds[0], (N_ISLAND, ISLAND_TOK, D), 1.0, 6.0, ((0, 4), (1, 8)))
    cotangent = normal_values(seeds[1], (N_ISLAND, ISLAND_TOK, KV_HEADS * HEAD), 1.0, 6.0, ((0, 4), (1, 8)))
    key_weight = normal_values(seeds[2], (N_ISLAND, D, KV_HEADS * HEAD), D ** -0.5, 0.0625, ((0, 4), (1, 8)))
    quant_codes = place_ends(jax.random.randint(seeds[3], (N_ISLAND, FRAG, D), 0, 16), jax.random.fold_in(seeds[3], 1), 0, 15).astype(jnp.int32)
    zero_points = place_ends(jax.random.randint(seeds[4], (N_ISLAND, FRAG, GROUPS), 0, 16), jax.random.fold_in(seeds[4], 1), 0, 15).astype(jnp.int32)
    minima = jnp.clip(jax.random.uniform(seeds[5], (N_ISLAND, FRAG, GROUPS), jnp.float32, -0.5, 0.5) * levels(seeds[5], (N_ISLAND, FRAG, GROUPS), ((0, 4), (1, 8)), -0.4, 0.0), -0.5, 0.5)
    quant_steps = jnp.clip(jnp.exp(math.log(0.1) - 2.3025851 * jax.random.uniform(seeds[6], (N_ISLAND, FRAG, GROUPS), jnp.float32) ** levels(seeds[6], (N_ISLAND, FRAG, GROUPS), ((0, 4), (1, 8)), -0.2, 0.2)), 0.01, 0.1)
    momentum = normal_values(seeds[7], (FRAG, D), 0.5, 4.0, ((0, 8),), jnp.float32)
    params = normal_values(seeds[8], (FRAG, D), 1.0, 6.0, ((0, 8),), jnp.float32)
    return {"tokens": tokens, "cotangent": cotangent, "key_weight": key_weight, "quant_codes": quant_codes, "zero_points": zero_points, "minima": minima, "quant_steps": quant_steps, "momentum": momentum, "params": params}


def dequantize(quant_codes, zero_points, minima, quant_steps):
    shape = quant_codes.shape
    grouped = quant_codes.reshape(shape[:-1] + (shape[-1] // GROUP, GROUP))
    offset = (grouped - zero_points[..., None]).astype(jnp.float32)
    values = quant_steps[..., None] * offset + minima[..., None]
    return values.reshape(shape)

def island_step(block):
    inputs, cot_rows, weight = block
    keys = jnp.dot(inputs, weight, preferred_element_type=jnp.float32).astype(jnp.bfloat16)
    back = jnp.dot(cot_rows, weight.T, preferred_element_type=jnp.float32).astype(jnp.bfloat16)
    grad = jnp.dot(inputs.T, cot_rows, preferred_element_type=jnp.float32) * (1.0 / math.sqrt(ISLAND_TOK))
    return (keys, back, grad)

def reference(tokens, cotangent, key_weight, quant_codes, zero_points, minima, quant_steps, momentum, params):
    projected, token_grad, weight_grad = lax.map(island_step, (tokens, cotangent, key_weight))
    values = dequantize(quant_codes, zero_points, minima, quant_steps)
    delta = lax.optimization_barrier(jnp.sum(values, axis=0)) / N_ISLAND
    new_momentum = 0.9 * momentum + delta
    new_params = params - 0.7 * (delta + 0.9 * new_momentum)
    return (projected, token_grad, weight_grad, new_momentum, new_params)
```

```python
import functools
import math

import jax
import jax.numpy as jnp
from jax import lax
from jax.experimental import pallas as pl
from jax.experimental.pallas import tpu as pltpu
from jax.sharding import PartitionSpec as P

GROUP = 128
MESH = pl.DeviceIdType.MESH
F32 = jnp.float32
BF16 = jnp.bfloat16
NZ = 4


def dequantize(quant_codes, zero_points, minima, quant_steps):
    shape = quant_codes.shape
    grouped = quant_codes.reshape(shape[:-1] + (shape[-1] // GROUP, GROUP))
    offset = (grouped - zero_points[..., None]).astype(F32)
    values = quant_steps[..., None] * offset + minima[..., None]
    return values.reshape(shape)


def local(
    tokens, cotangent, key_weight, quant_codes, zero_points, minima, quant_steps, momentum, params
):
    inputs = tokens[0]
    cot_rows = cotangent[0]
    weight = key_weight[0]
    island_tok = inputs.shape[0] * lax.axis_size("fsdp")
    scaling = 1.0 / math.sqrt(island_tok)
    piece = lax.all_gather(weight, "fsdp", axis=0, tiled=True)
    projected = jnp.dot(inputs, piece, preferred_element_type=F32).astype(BF16)
    back_acc = lax.dot_general(
        cot_rows, piece, (((1,), (1,)), ((), ())), preferred_element_type=F32
    ).astype(BF16)
    grad = lax.psum_scatter(
        lax.dot_general(inputs, cot_rows, (((0,), (0,)), ((), ())), preferred_element_type=F32),
        "fsdp",
        scatter_dimension=0,
        tiled=True,
    )
    weight_grad = grad * scaling
    values = dequantize(quant_codes[0], zero_points[0], minima[0], quant_steps[0])
    replicas = lax.axis_size("island")
    summed = lax.psum(values.astype(BF16), "island").astype(F32)
    delta = summed / replicas
    new_momentum = 0.9 * momentum + delta
    new_params = params - 0.7 * (delta + 0.9 * new_momentum)
    return (projected[None], back_acc[None], weight_grad[None], new_momentum, new_params)


def kernel(
    islands, rows_a, scaling,
    tok_hbm, cot_ref, w_hbm, codes_ref, zp_ref, min_ref, step_ref, mom_ref, par_ref,
    proj_ref, tg_ref, wg_ref, nmom_ref, npar_ref,
    tok, wf, part, xr_a, up_a, dn_a, up_b, dn_b, xr_b, vals, acc,
    in_sem, ga_up, ga_dn, ga_r, gax_s, gax_r, gbx, gb_up, gb_dn, gb_r,
    sax_s, sax_r, sa_s, sa_up, sa_dn, sb_s, sb_up, sb_dn, sbx, val_s, val_r,
):
    me = lax.axis_index("fsdp")
    isl = lax.axis_index("island")
    z, x = me // 2, me % 2
    ox = 1 - x
    rows = w_hbm.shape[0]
    A = pl.ds(0, rows_a)
    B = pl.ds(rows_a, rows - rows_a)
    flip = {"fsdp": me + 1 - 2 * x}
    above = {"fsdp": me + 2}
    below = {"fsdp": me - 2}
    has_up = z < NZ - 1
    has_dn = z > 0

    pending = []

    def send(make, to, cond=None):
        def copy():
            src, dst, ssem, rsem = make()
            return pltpu.make_async_remote_copy(
                src_ref=src, dst_ref=dst, send_sem=ssem, recv_sem=rsem,
                device_id=to, device_id_type=MESH)
        pending.append((cond, copy))
        copy().start()

    def arrived(dst, rsem):
        pltpu.make_async_remote_copy(
            src_ref=dst, dst_ref=dst, send_sem=rsem, recv_sem=rsem,
            device_id=flip, device_id_type=MESH).wait_recv()

    tok_in = pltpu.make_async_copy(tok_hbm, tok, in_sem.at[0])
    w_in = pltpu.make_async_copy(w_hbm, wf.at[z, x], in_sem.at[1])
    w_in.start()
    tok_in.start()

    barrier = pltpu.get_barrier_semaphore()
    pl.semaphore_signal(barrier, inc=1, device_id=flip, device_id_type=MESH)

    @pl.when(has_up)
    def _():
        pl.semaphore_signal(barrier, inc=1, device_id=above, device_id_type=MESH)

    @pl.when(has_dn)
    def _():
        pl.semaphore_signal(barrier, inc=1, device_id=below, device_id_type=MESH)

    for hop in range(1, islands):
        pl.semaphore_signal(
            barrier, inc=1, device_id={"island": (isl + hop) % islands}, device_id_type=MESH)
    pl.semaphore_wait(barrier, islands + has_up.astype(jnp.int32) + has_dn.astype(jnp.int32))

    def ga_send(zo, up, dn):
        c_up = jnp.logical_and(has_up, up)
        c_dn = jnp.logical_and(has_dn, dn)

        @pl.when(c_up)
        def _():
            send(lambda: (wf.at[zo, x, A], wf.at[zo, x, A], ga_up.at[zo], ga_r.at[zo]), above, c_up)

        @pl.when(c_dn)
        def _():
            send(lambda: (wf.at[zo, x, A], wf.at[zo, x, A], ga_dn.at[zo], ga_r.at[zo]), below, c_dn)

    def gax_send(zo, cond):
        send(lambda: (wf.at[zo, x, A], wf.at[zo, x, A], gax_s.at[zo], gax_r.at[zo]), flip, cond)

    def gb_send(zo, xo, up, dn):
        c_up = jnp.logical_and(has_up, up)
        c_dn = jnp.logical_and(has_dn, dn)

        @pl.when(c_up)
        def _():
            send(lambda: (wf.at[zo, xo, B], wf.at[zo, xo, B], gb_up.at[zo, xo], gb_r.at[zo, xo]),
                 above, c_up)

        @pl.when(c_dn)
        def _():
            send(lambda: (wf.at[zo, xo, B], wf.at[zo, xo, B], gb_dn.at[zo, xo], gb_r.at[zo, xo]),
                 below, c_dn)

    w_in.wait()
    send(lambda: (wf.at[z, x, B], wf.at[z, x, B], gbx.at[0], gbx.at[1]), flip)
    ga_send(z, True, True)

    tok_in.wait()
    cot = cot_ref[...]

    def sb_send(zt, xo, up, cond):
        if up:
            send(lambda: (part.at[zt, xo, B], up_b.at[zt, xo], sb_s.at[zt, xo], sb_up.at[zt, xo]),
                 above, cond)
        else:
            send(lambda: (part.at[zt, xo, B], dn_b.at[zt, xo], sb_s.at[zt, xo], sb_dn.at[zt, xo]),
                 below, cond)

    tile = 256
    tiles = rows // tile
    for zt in (NZ - 1, 0, 2, 1):
        def grad_tile(i, carry, zt=zt):
            xo, r = i // tiles, (i % tiles) * tile
            cols = pl.ds(pl.multiple_of((zt * 2 + xo) * rows + r, tile), tile)
            part[zt, xo, pl.ds(pl.multiple_of(r, tile), tile), :] = lax.dot_general(
                tok[:, cols], cot, (((0,), (0,)), ((), ())), preferred_element_type=F32
            ).astype(BF16)
            return carry

        lax.fori_loop(0, 2 * tiles, grad_tile, 0)
        send(lambda zt=zt: (part.at[zt, ox, A], xr_a.at[zt], sax_s.at[zt], sax_r.at[zt]), flip)
        if zt > 0:
            c0 = z == 0

            @pl.when(c0)
            def _(zt=zt):
                for xo in range(2):
                    sb_send(zt, xo, True, c0)
        if zt < NZ - 1:
            c3 = z == NZ - 1

            @pl.when(c3)
            def _(zt=zt):
                for xo in range(2):
                    sb_send(zt, xo, False, c3)

    for g in range(zp_ref.shape[1]):
        span = slice(g * GROUP, (g + 1) * GROUP)
        one = slice(g, g + 1)
        offset = (codes_ref[:, span] - zp_ref[:, one]).astype(F32)
        vals[isl, :, span] = (step_ref[:, one] * offset + min_ref[:, one]).astype(BF16)
    for hop in range(1, islands):
        send(lambda hop=hop: (vals.at[isl], vals.at[isl], val_s.at[hop - 1], val_r.at[isl]),
             {"island": (isl + hop) % islands})

    acc[...] = jnp.zeros_like(acc)

    def use(zo, xo, first, count):
        def body(i, carry):
            r = pl.multiple_of(first + i * 128, 128)
            cols = pl.ds(pl.multiple_of((zo * 2 + xo) * rows + r, 128), 128)
            block = wf[zo, xo, pl.ds(r, 128), :]
            acc[...] += jnp.dot(tok[:, cols], block, preferred_element_type=F32)
            tg_ref[:, cols] = lax.dot_general(
                cot_ref[...], block, (((1,), (1,)), ((), ())), preferred_element_type=F32
            ).astype(BF16)
            return carry

        lax.fori_loop(0, count // 128, body, 0)

    def use_a(zo, xo):
        use(zo, xo, 0, rows_a)

    def use_b(zo, xo):
        use(zo, xo, rows_a, rows - rows_a)

    def add(write, reads, count):
        def body(i, carry):
            here = pl.ds(pl.multiple_of(i * 64, 64), 64)
            total = reads[0][here, :].astype(F32)
            for ref in reads[1:]:
                total += ref[here, :].astype(F32)
            write(here, total)
            return carry

        lax.fori_loop(0, count // 64, body, 0)

    def into(ref):
        def write(here, total):
            ref[here, :] = total.astype(BF16)
        return write

    gax_send(z, None)
    use(z, x, 0, rows)

    def gb_open():
        arrived(wf.at[z, ox, B], gbx.at[1])
        gb_send(z, x, True, True)
        gb_send(z, ox, True, True)

    rows_b = rows - rows_a

    for t in range(1, NZ):
        for zo, ok, up in ((z - t, z - t >= 0, True), (z + t, z + t < NZ, False)):
            @pl.when(ok)
            def _(zo=zo, ok=ok):
                arrived(wf.at[zo, x, A], ga_r.at[zo])
            if up:
                ga_send(zo, ok, False)
            else:
                ga_send(zo, False, ok)

            @pl.when(ok)
            def _(zo=zo, ok=ok):
                gax_send(zo, ok)

        zt = NZ - 1 - t + z
        c = jnp.logical_and(has_dn, zt < NZ)
        go = jnp.logical_and(c, zt > z)

        @pl.when(go)
        def _(zt=zt, go=go):
            for xo in range(2):
                arrived(up_b.at[zt, xo], sb_up.at[zt, xo])
                add(into(part.at[zt, xo, B]), [part.at[zt, xo, B], up_b.at[zt, xo]], rows_b)
                sb_send(zt, xo, True, go)

        zd = t + z - (NZ - 1)
        c = jnp.logical_and(has_up, zd >= 0)
        gd = jnp.logical_and(c, zd < z)

        @pl.when(gd)
        def _(zd=zd, gd=gd):
            for xo in range(2):
                arrived(dn_b.at[zd, xo], sb_dn.at[zd, xo])
                add(into(part.at[zd, xo, B]), [part.at[zd, xo, B], dn_b.at[zd, xo]], rows_b)
                sb_send(zd, xo, False, gd)

        if t == 1:
            gb_open()
            use_b(z, ox)
        for zo, ok in ((z - t, z - t >= 0), (z + t, z + t < NZ)):
            @pl.when(ok)
            def _(zo=zo):
                use_a(zo, x)

    def b_sums(xo, write):
        own = part.at[z, xo, B]

        @pl.when(has_dn)
        def _():
            arrived(up_b.at[z, xo], sb_up.at[z, xo])

        @pl.when(has_up)
        def _():
            arrived(dn_b.at[z, xo], sb_dn.at[z, xo])

        @pl.when(jnp.logical_and(has_dn, has_up))
        def _():
            add(write, [own, up_b.at[z, xo], dn_b.at[z, xo]], rows_b)

        @pl.when(jnp.logical_not(has_dn))
        def _():
            add(write, [own, dn_b.at[z, xo]], rows_b)

        @pl.when(jnp.logical_not(has_up))
        def _():
            add(write, [own, up_b.at[z, xo]], rows_b)

    def wg_b(here, total):
        wg_ref[pl.ds(pl.multiple_of(rows_a + here.start, 64), 64), :] = total

    def sa_send(zt, up, cond):
        if up:
            send(lambda: (part.at[zt, x, A], up_a.at[zt], sa_s.at[zt], sa_up.at[zt]), above, cond)
        else:
            send(lambda: (part.at[zt, x, A], dn_a.at[zt], sa_s.at[zt], sa_dn.at[zt]), below, cond)

    for zt in (NZ - 1, 0, 2, 1):
        arrived(xr_a.at[zt], sax_r.at[zt])
        edge = []
        if zt > 0:
            edge.append((z == 0, True))
        if zt < NZ - 1:
            edge.append((z == NZ - 1, False))
        for c, up in edge:
            @pl.when(c)
            def _(zt=zt, c=c, up=up):
                add(into(part.at[zt, x, A]), [part.at[zt, x, A], xr_a.at[zt]], rows_a)
                sa_send(zt, up, c)

    b_sums(ox, into(part.at[z, ox, B]))
    send(lambda: (part.at[z, ox, B], xr_b, sbx.at[0], sbx.at[1]), flip)
    b_sums(x, wg_b)

    arrived(wf.at[z, ox, A], gax_r.at[z])
    use_a(z, ox)

    for hop in range(1, islands):
        other = (isl + hop) % islands
        arrived(vals.at[other], val_r.at[other])

    width = codes_ref.shape[1]

    def outer(i, carry):
        span = pl.ds(pl.multiple_of(i * 512, 512), 512)
        total = vals[0, :, span].astype(F32)
        for j in range(1, islands):
            total += vals[j, :, span].astype(F32)
        delta = total / islands
        new = 0.9 * mom_ref[:, span] + delta
        nmom_ref[:, span] = new
        npar_ref[:, span] = par_ref[:, span] - 0.7 * (delta + 0.9 * new)
        return carry

    lax.fori_loop(0, width // 512, outer, 0)

    for t in range(1, NZ):
        zt = NZ - 1 - t + z
        go = jnp.logical_and(jnp.logical_and(has_dn, zt < NZ), zt > z)

        @pl.when(go)
        def _(zt=zt, go=go):
            arrived(up_a.at[zt], sa_up.at[zt])
            add(into(part.at[zt, x, A]), [part.at[zt, x, A], xr_a.at[zt], up_a.at[zt]], rows_a)
            sa_send(zt, True, go)

        zd = t + z - (NZ - 1)
        gd = jnp.logical_and(jnp.logical_and(has_up, zd >= 0), zd < z)

        @pl.when(gd)
        def _(zd=zd, gd=gd):
            arrived(dn_a.at[zd], sa_dn.at[zd])
            add(into(part.at[zd, x, A]), [part.at[zd, x, A], xr_a.at[zd], dn_a.at[zd]], rows_a)
            sa_send(zd, False, gd)

        for zo, ok, up in ((z - t, z - t >= 0, True), (z + t, z + t < NZ, False)):
            for xo in range(2):
                @pl.when(ok)
                def _(zo=zo, xo=xo):
                    arrived(wf.at[zo, xo, B], gb_r.at[zo, xo])
                if up:
                    gb_send(zo, xo, ok, False)
                else:
                    gb_send(zo, xo, False, ok)

        for zo, ok in ((z - t, z - t >= 0), (z + t, z + t < NZ)):
            @pl.when(ok)
            def _(zo=zo):
                use_b(zo, 0)
                use_b(zo, 1)
                arrived(wf.at[zo, ox, A], gax_r.at[zo])
                use_a(zo, ox)

    proj_ref[...] = acc[...].astype(BF16)

    arrived(xr_b, sbx.at[1])

    def last_b(i, carry):
        here = pl.ds(pl.multiple_of(i * 64, 64), 64)
        there = pl.ds(pl.multiple_of(rows_a + i * 64, 64), 64)
        wg_ref[there, :] = (wg_ref[there, :] + xr_b[here, :].astype(F32)) * scaling
        return carry

    lax.fori_loop(0, rows_b // 64, last_b, 0)

    def wg_a(here, total):
        wg_ref[here, :] = total * scaling

    own = [part.at[z, x, A], xr_a.at[z]]

    @pl.when(has_dn)
    def _():
        arrived(up_a.at[z], sa_up.at[z])

    @pl.when(has_up)
    def _():
        arrived(dn_a.at[z], sa_dn.at[z])

    @pl.when(jnp.logical_and(has_dn, has_up))
    def _():
        add(wg_a, own + [up_a.at[z], dn_a.at[z]], rows_a)

    @pl.when(jnp.logical_not(has_dn))
    def _():
        add(wg_a, own + [dn_a.at[z]], rows_a)

    @pl.when(jnp.logical_not(has_up))
    def _():
        add(wg_a, own + [up_a.at[z]], rows_a)

    for cond, copy in pending:
        if cond is None:
            copy().wait_send()
        else:
            pl.when(cond)(lambda copy=copy: copy().wait_send())


def grid_local(
    islands,
    tokens, cotangent, key_weight, quant_codes, zero_points, minima, quant_steps, momentum, params
):
    tok_rows, width = tokens.shape[1:]
    rows, heads = key_weight.shape[1:]
    frag = quant_codes.shape[1]
    rows_a = rows // 128 * 5 // 8 * 128
    rows_b = rows - rows_a
    scaling = 1.0 / math.sqrt(tok_rows * 2 * NZ)
    vmem = pl.BlockSpec(memory_space=pltpu.VMEM)
    hbm = pl.BlockSpec(memory_space=pl.ANY)
    dma = pltpu.SemaphoreType.DMA
    outs = pl.pallas_call(
        functools.partial(kernel, islands, rows_a, scaling),
        out_shape=(
            jax.ShapeDtypeStruct((tok_rows, heads), BF16),
            jax.ShapeDtypeStruct((tok_rows, width), BF16),
            jax.ShapeDtypeStruct((rows, heads), F32),
            jax.ShapeDtypeStruct((frag, width), F32),
            jax.ShapeDtypeStruct((frag, width), F32),
        ),
        in_specs=[hbm, vmem, hbm] + [vmem] * 6,
        out_specs=[vmem] * 5,
        scratch_shapes=[
            pltpu.VMEM((tok_rows, width), BF16),
            pltpu.VMEM((NZ, 2, rows, heads), BF16),
            pltpu.VMEM((NZ, 2, rows, heads), BF16),
            pltpu.VMEM((NZ, rows_a, heads), BF16),
            pltpu.VMEM((NZ, rows_a, heads), BF16),
            pltpu.VMEM((NZ, rows_a, heads), BF16),
            pltpu.VMEM((NZ, 2, rows_b, heads), BF16),
            pltpu.VMEM((NZ, 2, rows_b, heads), BF16),
            pltpu.VMEM((rows_b, heads), BF16),
            pltpu.VMEM((islands, frag, width), BF16),
            pltpu.VMEM((tok_rows, heads), F32),
            dma((2,)),
            dma((NZ,)), dma((NZ,)), dma((NZ,)), dma((NZ,)), dma((NZ,)), dma((2,)),
            dma((NZ, 2)), dma((NZ, 2)), dma((NZ, 2)),
            dma((NZ,)), dma((NZ,)), dma((NZ,)), dma((NZ,)), dma((NZ,)),
            dma((NZ, 2)), dma((NZ, 2)), dma((NZ, 2)), dma((2,)),
            dma((islands - 1,)), dma((islands,)),
        ],
        compiler_params=pltpu.CompilerParams(
            collective_id=0, has_side_effects=True, vmem_limit_bytes=60 * 2**20
        ),
        cost_estimate=pl.CostEstimate(
            flops=6 * tok_rows * width * heads, bytes_accessed=20 * 2**20, transcendentals=0
        ),
    )(
        tokens[0], cotangent[0], key_weight[0], quant_codes[0], zero_points[0], minima[0],
        quant_steps[0], momentum, params,
    )
    projected, token_grad, weight_grad, new_momentum, new_params = outs
    return (projected[None], token_grad[None], weight_grad[None], new_momentum, new_params)


def solution(mesh):
    placed = (P("island", "fsdp", None),) * 7 + (P("fsdp", None),) * 2
    if mesh.shape["fsdp"] == 2 * NZ:
        body = functools.partial(grid_local, mesh.shape["island"])
    else:
        body = local
    return jax.shard_map(
        body,
        mesh=mesh,
        in_specs=placed,
        out_specs=(P("island", "fsdp", None),) * 3 + (P("fsdp", None),) * 2,
        check_vma=False,
    )
```

```python
import functools
import math

import jax
import jax.numpy as jnp
from jax import lax
from jax.experimental import pallas as pl
from jax.experimental.pallas import tpu as pltpu
from jax.sharding import PartitionSpec as P

GROUP = 128
MESH = pl.DeviceIdType.MESH
F32 = jnp.float32
BF16 = jnp.bfloat16
NZ = 4


def dequantize(quant_codes, zero_points, minima, quant_steps):
    shape = quant_codes.shape
    grouped = quant_codes.reshape(shape[:-1] + (shape[-1] // GROUP, GROUP))
    offset = (grouped - zero_points[..., None]).astype(F32)
    values = quant_steps[..., None] * offset + minima[..., None]
    return values.reshape(shape)


def local(
    tokens, cotangent, key_weight, quant_codes, zero_points, minima, quant_steps, momentum, params
):
    inputs = tokens[0]
    cot_rows = cotangent[0]
    weight = key_weight[0]
    island_tok = inputs.shape[0] * lax.axis_size("fsdp")
    scaling = 1.0 / math.sqrt(island_tok)
    piece = lax.all_gather(weight, "fsdp", axis=0, tiled=True)
    projected = jnp.dot(inputs, piece, preferred_element_type=F32).astype(BF16)
    back_acc = lax.dot_general(
        cot_rows, piece, (((1,), (1,)), ((), ())), preferred_element_type=F32
    ).astype(BF16)
    grad = lax.psum_scatter(
        lax.dot_general(inputs, cot_rows, (((0,), (0,)), ((), ())), preferred_element_type=F32),
        "fsdp",
        scatter_dimension=0,
        tiled=True,
    )
    weight_grad = grad * scaling
    values = dequantize(quant_codes[0], zero_points[0], minima[0], quant_steps[0])
    replicas = lax.axis_size("island")
    summed = lax.psum(values.astype(BF16), "island").astype(F32)
    delta = summed / replicas
    new_momentum = 0.9 * momentum + delta
    new_params = params - 0.7 * (delta + 0.9 * new_momentum)
    return (projected[None], back_acc[None], weight_grad[None], new_momentum, new_params)


def kernel(
    islands, rows_a, scaling,
    tok_hbm, cot_ref, w_hbm, codes_ref, zp_ref, min_ref, step_ref, mom_ref, par_ref,
    proj_ref, tg_ref, wg_ref, nmom_ref, npar_ref,
    tok, wf, part, xr_a, up_a, dn_a, up_b, dn_b, xr_b, vals, acc,
    in_sem, ga_up, ga_dn, ga_r, gax_s, gax_r, gbx, gb_up, gb_dn, gb_r,
    sax_s, sax_r, sa_s, sa_up, sa_dn, sb_s, sb_up, sb_dn, sbx, val_s, val_r,
):
    me = lax.axis_index("fsdp")
    isl = lax.axis_index("island")
    z, x = me // 2, me % 2
    ox = 1 - x
    rows = w_hbm.shape[0]
    A = pl.ds(0, rows_a)
    B = pl.ds(rows_a, rows - rows_a)
    flip = {"fsdp": me + 1 - 2 * x}
    above = {"fsdp": me + 2}
    below = {"fsdp": me - 2}
    has_up = z < NZ - 1
    has_dn = z > 0

    pending = []

    def send(make, to, cond=None, early=None):
        def copy():
            src, dst, ssem, rsem = make()
            return pltpu.make_async_remote_copy(
                src_ref=src, dst_ref=dst, send_sem=ssem, recv_sem=rsem,
                device_id=to, device_id_type=MESH)
        if early is not True:
            pending.append((cond, early, copy))
        copy().start()

    def arrived(dst, rsem):
        pltpu.make_async_remote_copy(
            src_ref=dst, dst_ref=dst, send_sem=rsem, recv_sem=rsem,
            device_id=flip, device_id_type=MESH).wait_recv()

    tok_in = pltpu.make_async_copy(tok_hbm, tok, in_sem.at[0])
    w_in = pltpu.make_async_copy(w_hbm, wf.at[z, x], in_sem.at[1])
    w_in.start()
    tok_in.start()

    barrier = pltpu.get_barrier_semaphore()
    pl.semaphore_signal(barrier, inc=1, device_id=flip, device_id_type=MESH)

    @pl.when(has_up)
    def _():
        pl.semaphore_signal(barrier, inc=1, device_id=above, device_id_type=MESH)

    @pl.when(has_dn)
    def _():
        pl.semaphore_signal(barrier, inc=1, device_id=below, device_id_type=MESH)

    for hop in range(1, islands):
        pl.semaphore_signal(
            barrier, inc=1, device_id={"island": (isl + hop) % islands}, device_id_type=MESH)
    pl.semaphore_wait(barrier, islands + has_up.astype(jnp.int32) + has_dn.astype(jnp.int32))

    first, last = z == 0, z == NZ - 1

    def ga_send(zo, up, dn, own=False):
        c_up = jnp.logical_and(has_up, up)
        c_dn = jnp.logical_and(has_dn, dn)

        @pl.when(c_up)
        def _():
            send(lambda: (wf.at[zo, x, A], wf.at[zo, x, A], ga_up.at[zo], ga_r.at[zo]), above, c_up,
                 first if own else None)

        @pl.when(c_dn)
        def _():
            send(lambda: (wf.at[zo, x, A], wf.at[zo, x, A], ga_dn.at[zo], ga_r.at[zo]), below, c_dn,
                 last if own else None)

    def gax_send(zo, cond):
        send(lambda: (wf.at[zo, x, A], wf.at[zo, x, A], gax_s.at[zo], gax_r.at[zo]), flip, cond)

    def gb_send(zo, xo, up, dn, own=False):
        c_up = jnp.logical_and(has_up, up)
        c_dn = jnp.logical_and(has_dn, dn)

        @pl.when(c_up)
        def _():
            send(lambda: (wf.at[zo, xo, B], wf.at[zo, xo, B], gb_up.at[zo, xo], gb_r.at[zo, xo]),
                 above, c_up, first if own else None)

        @pl.when(c_dn)
        def _():
            send(lambda: (wf.at[zo, xo, B], wf.at[zo, xo, B], gb_dn.at[zo, xo], gb_r.at[zo, xo]),
                 below, c_dn, last if own else None)

    w_in.wait()
    send(lambda: (wf.at[z, x, B], wf.at[z, x, B], gbx.at[0], gbx.at[1]), flip)
    ga_send(z, True, True, own=True)

    tok_in.wait()
    cot = cot_ref[...]

    def sb_send(zt, xo, up, cond, early=None):
        if up:
            send(lambda: (part.at[zt, xo, B], up_b.at[zt, xo], sb_s.at[zt, xo], sb_up.at[zt, xo]),
                 above, cond, early)
        else:
            send(lambda: (part.at[zt, xo, B], dn_b.at[zt, xo], sb_s.at[zt, xo], sb_dn.at[zt, xo]),
                 below, cond, early)

    def sent(make, to):
        src, dst, ssem, rsem = make()
        pltpu.make_async_remote_copy(
            src_ref=src, dst_ref=dst, send_sem=ssem, recv_sem=rsem,
            device_id=to, device_id_type=MESH).wait_send()

    def sb_start(t, up):
        end = 0 if up else NZ - 1
        zt = NZ - 1 - t if up else t
        c = z == end
        to = above if up else below

        @pl.when(c)
        def _():
            if t == 0:
                if up:
                    sent(lambda: (wf.at[z, x, A], wf.at[z, x, A], ga_up.at[z], ga_r.at[z]), to)
                else:
                    sent(lambda: (wf.at[z, x, A], wf.at[z, x, A], ga_dn.at[z], ga_r.at[z]), to)
            else:
                before = zt + 1 if up else zt - 1
                sent(lambda: (part.at[before, 0, B], up_b.at[before, 0], sb_s.at[before, 0],
                              sb_up.at[before, 0]), to)
            for xo in range(2):
                sb_send(zt, xo, up, c, True if xo == 0 and t < NZ - 2 else None)

    tile = 256
    tiles = rows // tile
    for zt in (NZ - 1, 0, 2, 1):
        def grad_tile(i, carry, zt=zt):
            xo, r = i // tiles, (i % tiles) * tile
            cols = pl.ds(pl.multiple_of((zt * 2 + xo) * rows + r, tile), tile)
            part[zt, xo, pl.ds(pl.multiple_of(r, tile), tile), :] = lax.dot_general(
                tok[:, cols], cot, (((0,), (0,)), ((), ())), preferred_element_type=F32
            ).astype(BF16)
            return carry

        lax.fori_loop(0, 2 * tiles, grad_tile, 0)
        send(lambda zt=zt: (part.at[zt, ox, A], xr_a.at[zt], sax_s.at[zt], sax_r.at[zt]), flip)

    for g in range(zp_ref.shape[1]):
        span = slice(g * GROUP, (g + 1) * GROUP)
        one = slice(g, g + 1)
        offset = (codes_ref[:, span] - zp_ref[:, one]).astype(F32)
        vals[isl, :, span] = (step_ref[:, one] * offset + min_ref[:, one]).astype(BF16)
    for hop in range(1, islands):
        send(lambda hop=hop: (vals.at[isl], vals.at[isl], val_s.at[hop - 1], val_r.at[isl]),
             {"island": (isl + hop) % islands})

    acc[...] = jnp.zeros_like(acc)

    def use(zo, xo, first, count):
        def body(i, carry):
            r = pl.multiple_of(first + i * 128, 128)
            cols = pl.ds(pl.multiple_of((zo * 2 + xo) * rows + r, 128), 128)
            block = wf[zo, xo, pl.ds(r, 128), :]
            acc[...] += jnp.dot(tok[:, cols], block, preferred_element_type=F32)
            tg_ref[:, cols] = lax.dot_general(
                cot_ref[...], block, (((1,), (1,)), ((), ())), preferred_element_type=F32
            ).astype(BF16)
            return carry

        lax.fori_loop(0, count // 128, body, 0)

    def use_a(zo, xo):
        use(zo, xo, 0, rows_a)

    def use_b(zo, xo):
        use(zo, xo, rows_a, rows - rows_a)

    def add(write, reads, count):
        def body(i, carry):
            here = pl.ds(pl.multiple_of(i * 64, 64), 64)
            total = reads[0][here, :].astype(F32)
            for ref in reads[1:]:
                total += ref[here, :].astype(F32)
            write(here, total)
            return carry

        lax.fori_loop(0, count // 64, body, 0)

    def into(ref):
        def write(here, total):
            ref[here, :] = total.astype(BF16)
        return write

    gax_send(z, None)
    sb_start(0, True)
    sb_start(0, False)
    use(z, x, 0, rows)

    def gb_open():
        arrived(wf.at[z, ox, B], gbx.at[1])
        gb_send(z, x, True, True, own=True)
        gb_send(z, ox, True, True)

    rows_b = rows - rows_a

    for t in range(1, NZ):
        for zo, ok, up in ((z - t, z - t >= 0, True), (z + t, z + t < NZ, False)):
            @pl.when(ok)
            def _(zo=zo, ok=ok):
                arrived(wf.at[zo, x, A], ga_r.at[zo])
            if up:
                ga_send(zo, ok, False)
            else:
                ga_send(zo, False, ok)

            @pl.when(ok)
            def _(zo=zo, ok=ok):
                gax_send(zo, ok)

        zt = NZ - 1 - t + z
        c = jnp.logical_and(has_dn, zt < NZ)
        go = jnp.logical_and(c, zt > z)

        @pl.when(go)
        def _(zt=zt, go=go):
            for xo in range(2):
                arrived(up_b.at[zt, xo], sb_up.at[zt, xo])
                add(into(part.at[zt, xo, B]), [part.at[zt, xo, B], up_b.at[zt, xo]], rows_b)
                sb_send(zt, xo, True, go)

        zd = t + z - (NZ - 1)
        c = jnp.logical_and(has_up, zd >= 0)
        gd = jnp.logical_and(c, zd < z)

        @pl.when(gd)
        def _(zd=zd, gd=gd):
            for xo in range(2):
                arrived(dn_b.at[zd, xo], sb_dn.at[zd, xo])
                add(into(part.at[zd, xo, B]), [part.at[zd, xo, B], dn_b.at[zd, xo]], rows_b)
                sb_send(zd, xo, False, gd)

        if t < NZ - 1:
            sb_start(t, True)
            sb_start(t, False)
        if t == NZ - 2:
            gb_open()
        for zo, ok in ((z - t, z - t >= 0), (z + t, z + t < NZ)):
            @pl.when(ok)
            def _(zo=zo):
                use_a(zo, x)

    def b_sums(xo, write):
        own = part.at[z, xo, B]

        @pl.when(has_dn)
        def _():
            arrived(up_b.at[z, xo], sb_up.at[z, xo])

        @pl.when(has_up)
        def _():
            arrived(dn_b.at[z, xo], sb_dn.at[z, xo])

        @pl.when(jnp.logical_and(has_dn, has_up))
        def _():
            add(write, [own, up_b.at[z, xo], dn_b.at[z, xo]], rows_b)

        @pl.when(jnp.logical_not(has_dn))
        def _():
            add(write, [own, dn_b.at[z, xo]], rows_b)

        @pl.when(jnp.logical_not(has_up))
        def _():
            add(write, [own, up_b.at[z, xo]], rows_b)

    def wg_b(here, total):
        wg_ref[pl.ds(pl.multiple_of(rows_a + here.start, 64), 64), :] = total

    def sa_send(zt, up, cond, early=None):
        if up:
            send(lambda: (part.at[zt, x, A], up_a.at[zt], sa_s.at[zt], sa_up.at[zt]), above, cond,
                 early)
        else:
            send(lambda: (part.at[zt, x, A], dn_a.at[zt], sa_s.at[zt], sa_dn.at[zt]), below, cond,
                 early)

    def sa_start(t, up):
        zt = NZ - 1 - t if up else t
        c = first if up else last
        to = above if up else below

        @pl.when(c)
        def _():
            add(into(part.at[zt, x, A]), [part.at[zt, x, A], xr_a.at[zt]], rows_a)
            if t == 0:
                if up:
                    sent(lambda: (wf.at[z, x, B], wf.at[z, x, B], gb_up.at[z, x], gb_r.at[z, x]), to)
                else:
                    sent(lambda: (wf.at[z, x, B], wf.at[z, x, B], gb_dn.at[z, x], gb_r.at[z, x]), to)
            else:
                before = zt + 1 if up else zt - 1
                sent(lambda: (part.at[before, x, A], up_a.at[before], sa_s.at[before],
                              sa_up.at[before]), to)
            sa_send(zt, up, c, True if t < NZ - 2 else None)

    for zt in (NZ - 1, 0, 2, 1):
        arrived(xr_a.at[zt], sax_r.at[zt])
    use_b(z, ox)
    sa_start(0, True)
    sa_start(0, False)

    b_sums(ox, into(part.at[z, ox, B]))
    send(lambda: (part.at[z, ox, B], xr_b, sbx.at[0], sbx.at[1]), flip)
    b_sums(x, wg_b)

    arrived(wf.at[z, ox, A], gax_r.at[z])
    use_a(z, ox)

    for hop in range(1, islands):
        other = (isl + hop) % islands
        arrived(vals.at[other], val_r.at[other])

    width = codes_ref.shape[1]

    def outer(i, carry):
        span = pl.ds(pl.multiple_of(i * 512, 512), 512)
        total = vals[0, :, span].astype(F32)
        for j in range(1, islands):
            total += vals[j, :, span].astype(F32)
        delta = total / islands
        new = 0.9 * mom_ref[:, span] + delta
        nmom_ref[:, span] = new
        npar_ref[:, span] = par_ref[:, span] - 0.7 * (delta + 0.9 * new)
        return carry

    lax.fori_loop(0, width // 512, outer, 0)

    for t in range(1, NZ):
        for zo, ok, up in ((z - t, z - t >= 0, True), (z + t, z + t < NZ, False)):
            for xo in range(2):
                @pl.when(ok)
                def _(zo=zo, xo=xo):
                    arrived(wf.at[zo, xo, B], gb_r.at[zo, xo])
                if up:
                    gb_send(zo, xo, ok, False)
                else:
                    gb_send(zo, xo, False, ok)

        zt = NZ - 1 - t + z
        go = jnp.logical_and(jnp.logical_and(has_dn, zt < NZ), zt > z)

        @pl.when(go)
        def _(zt=zt, go=go):
            arrived(up_a.at[zt], sa_up.at[zt])
            add(into(part.at[zt, x, A]), [part.at[zt, x, A], xr_a.at[zt], up_a.at[zt]], rows_a)
            sa_send(zt, True, go)

        zd = t + z - (NZ - 1)
        gd = jnp.logical_and(jnp.logical_and(has_up, zd >= 0), zd < z)

        @pl.when(gd)
        def _(zd=zd, gd=gd):
            arrived(dn_a.at[zd], sa_dn.at[zd])
            add(into(part.at[zd, x, A]), [part.at[zd, x, A], xr_a.at[zd], dn_a.at[zd]], rows_a)
            sa_send(zd, False, gd)

        if t < NZ - 1:
            sa_start(t, True)
            sa_start(t, False)

        for zo, ok in ((z - t, z - t >= 0), (z + t, z + t < NZ)):
            @pl.when(ok)
            def _(zo=zo):
                use_b(zo, 0)
                use_b(zo, 1)
                arrived(wf.at[zo, ox, A], gax_r.at[zo])
                use_a(zo, ox)

    proj_ref[...] = acc[...].astype(BF16)

    arrived(xr_b, sbx.at[1])

    def last_b(i, carry):
        here = pl.ds(pl.multiple_of(i * 64, 64), 64)
        there = pl.ds(pl.multiple_of(rows_a + i * 64, 64), 64)
        wg_ref[there, :] = (wg_ref[there, :] + xr_b[here, :].astype(F32)) * scaling
        return carry

    lax.fori_loop(0, rows_b // 64, last_b, 0)

    def wg_a(here, total):
        wg_ref[here, :] = total * scaling

    own = [part.at[z, x, A], xr_a.at[z]]

    @pl.when(has_dn)
    def _():
        arrived(up_a.at[z], sa_up.at[z])

    @pl.when(has_up)
    def _():
        arrived(dn_a.at[z], sa_dn.at[z])

    @pl.when(jnp.logical_and(has_dn, has_up))
    def _():
        add(wg_a, own + [up_a.at[z], dn_a.at[z]], rows_a)

    @pl.when(jnp.logical_not(has_dn))
    def _():
        add(wg_a, own + [dn_a.at[z]], rows_a)

    @pl.when(jnp.logical_not(has_up))
    def _():
        add(wg_a, own + [up_a.at[z]], rows_a)

    for cond, early, copy in pending:
        if early is not None:
            cond = jnp.logical_and(cond, jnp.logical_not(early))
        if cond is None:
            copy().wait_send()
        else:
            pl.when(cond)(lambda copy=copy: copy().wait_send())


def grid_local(
    islands,
    tokens, cotangent, key_weight, quant_codes, zero_points, minima, quant_steps, momentum, params
):
    tok_rows, width = tokens.shape[1:]
    rows, heads = key_weight.shape[1:]
    frag = quant_codes.shape[1]
    rows_a = rows // 128 * 5 // 8 * 128
    rows_b = rows - rows_a
    scaling = 1.0 / math.sqrt(tok_rows * 2 * NZ)
    vmem = pl.BlockSpec(memory_space=pltpu.VMEM)
    hbm = pl.BlockSpec(memory_space=pl.ANY)
    dma = pltpu.SemaphoreType.DMA
    outs = pl.pallas_call(
        functools.partial(kernel, islands, rows_a, scaling),
        out_shape=(
            jax.ShapeDtypeStruct((tok_rows, heads), BF16),
            jax.ShapeDtypeStruct((tok_rows, width), BF16),
            jax.ShapeDtypeStruct((rows, heads), F32),
            jax.ShapeDtypeStruct((frag, width), F32),
            jax.ShapeDtypeStruct((frag, width), F32),
        ),
        in_specs=[hbm, vmem, hbm] + [vmem] * 6,
        out_specs=[vmem] * 5,
        scratch_shapes=[
            pltpu.VMEM((tok_rows, width), BF16),
            pltpu.VMEM((NZ, 2, rows, heads), BF16),
            pltpu.VMEM((NZ, 2, rows, heads), BF16),
            pltpu.VMEM((NZ, rows_a, heads), BF16),
            pltpu.VMEM((NZ, rows_a, heads), BF16),
            pltpu.VMEM((NZ, rows_a, heads), BF16),
            pltpu.VMEM((NZ, 2, rows_b, heads), BF16),
            pltpu.VMEM((NZ, 2, rows_b, heads), BF16),
            pltpu.VMEM((rows_b, heads), BF16),
            pltpu.VMEM((islands, frag, width), BF16),
            pltpu.VMEM((tok_rows, heads), F32),
            dma((2,)),
            dma((NZ,)), dma((NZ,)), dma((NZ,)), dma((NZ,)), dma((NZ,)), dma((2,)),
            dma((NZ, 2)), dma((NZ, 2)), dma((NZ, 2)),
            dma((NZ,)), dma((NZ,)), dma((NZ,)), dma((NZ,)), dma((NZ,)),
            dma((NZ, 2)), dma((NZ, 2)), dma((NZ, 2)), dma((2,)),
            dma((islands - 1,)), dma((islands,)),
        ],
        compiler_params=pltpu.CompilerParams(
            collective_id=0, has_side_effects=True, vmem_limit_bytes=60 * 2**20
        ),
        cost_estimate=pl.CostEstimate(
            flops=6 * tok_rows * width * heads, bytes_accessed=20 * 2**20, transcendentals=0
        ),
    )(
        tokens[0], cotangent[0], key_weight[0], quant_codes[0], zero_points[0], minima[0],
        quant_steps[0], momentum, params,
    )
    projected, token_grad, weight_grad, new_momentum, new_params = outs
    return (projected[None], token_grad[None], weight_grad[None], new_momentum, new_params)


def solution(mesh):
    placed = (P("island", "fsdp", None),) * 7 + (P("fsdp", None),) * 2
    if mesh.shape["fsdp"] == 2 * NZ:
        body = functools.partial(grid_local, mesh.shape["island"])
    else:
        body = local
    return jax.shard_map(
        body,
        mesh=mesh,
        in_specs=placed,
        out_specs=(P("island", "fsdp", None),) * 3 + (P("fsdp", None),) * 2,
        check_vma=False,
    )
```

```python
import functools
import math

import jax
import jax.numpy as jnp
from jax import lax
from jax.experimental import pallas as pl
from jax.experimental.pallas import tpu as pltpu
from jax.sharding import PartitionSpec as P

GROUP = 128
MESH = pl.DeviceIdType.MESH
F32 = jnp.float32
BF16 = jnp.bfloat16
NZ = 4


def dequantize(quant_codes, zero_points, minima, quant_steps):
    shape = quant_codes.shape
    grouped = quant_codes.reshape(shape[:-1] + (shape[-1] // GROUP, GROUP))
    offset = (grouped - zero_points[..., None]).astype(F32)
    values = quant_steps[..., None] * offset + minima[..., None]
    return values.reshape(shape)


def local(
    tokens, cotangent, key_weight, quant_codes, zero_points, minima, quant_steps, momentum, params
):
    inputs = tokens[0]
    cot_rows = cotangent[0]
    weight = key_weight[0]
    island_tok = inputs.shape[0] * lax.axis_size("fsdp")
    scaling = 1.0 / math.sqrt(island_tok)
    piece = lax.all_gather(weight, "fsdp", axis=0, tiled=True)
    projected = jnp.dot(inputs, piece, preferred_element_type=F32).astype(BF16)
    back_acc = lax.dot_general(
        cot_rows, piece, (((1,), (1,)), ((), ())), preferred_element_type=F32
    ).astype(BF16)
    grad = lax.psum_scatter(
        lax.dot_general(inputs, cot_rows, (((0,), (0,)), ((), ())), preferred_element_type=F32),
        "fsdp",
        scatter_dimension=0,
        tiled=True,
    )
    weight_grad = grad * scaling
    values = dequantize(quant_codes[0], zero_points[0], minima[0], quant_steps[0])
    replicas = lax.axis_size("island")
    summed = lax.psum(values.astype(BF16), "island").astype(F32)
    delta = summed / replicas
    new_momentum = 0.9 * momentum + delta
    new_params = params - 0.7 * (delta + 0.9 * new_momentum)
    return (projected[None], back_acc[None], weight_grad[None], new_momentum, new_params)


def kernel(
    islands, rows_a, scaling,
    tok_hbm, cot_hbm, w_hbm, codes_hbm, zp_hbm, min_hbm, step_hbm, mom_hbm, par_hbm,
    proj_ref, tg_ref, wg_ref, nmom_ref, npar_ref,
    tok, cot_ref, codes_ref, zp_ref, min_ref, step_ref, mom_ref, par_ref, wf, part, xr_a, up_a, dn_a, up_b, dn_b, xr_b, vals, acc,
    in_sem, ga_up, ga_dn, ga_r, gax_s, gax_r, gbx, gb_up, gb_dn, gb_r,
    sax_s, sax_r, sa_s, sa_up, sa_dn, sb_s, sb_up, sb_dn, sbx, val_s, val_r,
):
    me = lax.axis_index("fsdp")
    isl = lax.axis_index("island")
    z, x = me // 2, me % 2
    ox = 1 - x
    rows = w_hbm.shape[0]
    A = pl.ds(0, rows_a)
    B = pl.ds(rows_a, rows - rows_a)
    flip = {"fsdp": me + 1 - 2 * x}
    above = {"fsdp": me + 2}
    below = {"fsdp": me - 2}
    has_up = z < NZ - 1
    has_dn = z > 0

    pending = []

    def send(make, to, cond=None, early=None):
        def copy():
            src, dst, ssem, rsem = make()
            return pltpu.make_async_remote_copy(
                src_ref=src, dst_ref=dst, send_sem=ssem, recv_sem=rsem,
                device_id=to, device_id_type=MESH)
        if early is not True:
            pending.append((cond, early, copy))
        copy().start()

    def arrived(dst, rsem):
        pltpu.make_async_remote_copy(
            src_ref=dst, dst_ref=dst, send_sem=rsem, recv_sem=rsem,
            device_id=flip, device_id_type=MESH).wait_recv()

    tok_in = pltpu.make_async_copy(tok_hbm, tok, in_sem.at[0])
    w_in = pltpu.make_async_copy(w_hbm, wf.at[z, x], in_sem.at[1])
    cot_in = pltpu.make_async_copy(cot_hbm, cot_ref, in_sem.at[2])
    quant_in = [
        pltpu.make_async_copy(src, dst, in_sem.at[3 + i])
        for i, (src, dst) in enumerate((
            (codes_hbm, codes_ref), (zp_hbm, zp_ref), (min_hbm, min_ref), (step_hbm, step_ref),
            (mom_hbm, mom_ref), (par_hbm, par_ref)))
    ]
    w_in.start()
    cot_in.start()
    tok_in.start()
    for copy in quant_in:
        copy.start()

    barrier = pltpu.get_barrier_semaphore()
    pl.semaphore_signal(barrier, inc=1, device_id=flip, device_id_type=MESH)

    @pl.when(has_up)
    def _():
        pl.semaphore_signal(barrier, inc=1, device_id=above, device_id_type=MESH)

    @pl.when(has_dn)
    def _():
        pl.semaphore_signal(barrier, inc=1, device_id=below, device_id_type=MESH)

    for hop in range(1, islands):
        pl.semaphore_signal(
            barrier, inc=1, device_id={"island": (isl + hop) % islands}, device_id_type=MESH)
    pl.semaphore_wait(barrier, islands + has_up.astype(jnp.int32) + has_dn.astype(jnp.int32))

    first, last = z == 0, z == NZ - 1

    def ga_send(zo, up, dn, own=False):
        c_up = jnp.logical_and(has_up, up)
        c_dn = jnp.logical_and(has_dn, dn)

        @pl.when(c_up)
        def _():
            send(lambda: (wf.at[zo, x, A], wf.at[zo, x, A], ga_up.at[zo], ga_r.at[zo]), above, c_up,
                 first if own else None)

        @pl.when(c_dn)
        def _():
            send(lambda: (wf.at[zo, x, A], wf.at[zo, x, A], ga_dn.at[zo], ga_r.at[zo]), below, c_dn,
                 last if own else None)

    def gax_send(zo, cond):
        send(lambda: (wf.at[zo, x, A], wf.at[zo, x, A], gax_s.at[zo], gax_r.at[zo]), flip, cond)

    def gb_send(zo, xo, up, dn, own=False):
        c_up = jnp.logical_and(has_up, up)
        c_dn = jnp.logical_and(has_dn, dn)

        @pl.when(c_up)
        def _():
            send(lambda: (wf.at[zo, xo, B], wf.at[zo, xo, B], gb_up.at[zo, xo], gb_r.at[zo, xo]),
                 above, c_up, first if own else None)

        @pl.when(c_dn)
        def _():
            send(lambda: (wf.at[zo, xo, B], wf.at[zo, xo, B], gb_dn.at[zo, xo], gb_r.at[zo, xo]),
                 below, c_dn, last if own else None)

    w_in.wait()
    send(lambda: (wf.at[z, x, B], wf.at[z, x, B], gbx.at[0], gbx.at[1]), flip)
    ga_send(z, True, True, own=True)

    cot_in.wait()
    tok_in.wait()
    cot = cot_ref[...]

    def sb_send(zt, xo, up, cond, early=None):
        if up:
            send(lambda: (part.at[zt, xo, B], up_b.at[zt, xo], sb_s.at[zt, xo], sb_up.at[zt, xo]),
                 above, cond, early)
        else:
            send(lambda: (part.at[zt, xo, B], dn_b.at[zt, xo], sb_s.at[zt, xo], sb_dn.at[zt, xo]),
                 below, cond, early)

    def sent(make, to):
        src, dst, ssem, rsem = make()
        pltpu.make_async_remote_copy(
            src_ref=src, dst_ref=dst, send_sem=ssem, recv_sem=rsem,
            device_id=to, device_id_type=MESH).wait_send()

    def sb_start(t, up):
        end = 0 if up else NZ - 1
        zt = NZ - 1 - t if up else t
        c = z == end
        to = above if up else below

        @pl.when(c)
        def _():
            if t == 0:
                if up:
                    sent(lambda: (wf.at[z, x, A], wf.at[z, x, A], ga_up.at[z], ga_r.at[z]), to)
                else:
                    sent(lambda: (wf.at[z, x, A], wf.at[z, x, A], ga_dn.at[z], ga_r.at[z]), to)
            else:
                before = zt + 1 if up else zt - 1
                sent(lambda: (part.at[before, 0, B], up_b.at[before, 0], sb_s.at[before, 0],
                              sb_up.at[before, 0]), to)
            for xo in range(2):
                sb_send(zt, xo, up, c, True if xo == 0 and t < NZ - 2 else None)

    tile = 256
    tiles = rows // tile
    for zt in (NZ - 1, 0, 2, 1):
        def grad_tile(i, carry, zt=zt):
            xo, r = i // tiles, (i % tiles) * tile
            cols = pl.ds(pl.multiple_of((zt * 2 + xo) * rows + r, tile), tile)
            part[zt, xo, pl.ds(pl.multiple_of(r, tile), tile), :] = lax.dot_general(
                tok[:, cols], cot, (((0,), (0,)), ((), ())), preferred_element_type=F32
            ).astype(BF16)
            return carry

        lax.fori_loop(0, 2 * tiles, grad_tile, 0)
        send(lambda zt=zt: (part.at[zt, ox, A], xr_a.at[zt], sax_s.at[zt], sax_r.at[zt]), flip)

    for copy in quant_in:
        copy.wait()

    for g in range(zp_ref.shape[1]):
        span = slice(g * GROUP, (g + 1) * GROUP)
        one = slice(g, g + 1)
        offset = (codes_ref[:, span] - zp_ref[:, one]).astype(F32)
        vals[isl, :, span] = (step_ref[:, one] * offset + min_ref[:, one]).astype(BF16)
    for hop in range(1, islands):
        send(lambda hop=hop: (vals.at[isl], vals.at[isl], val_s.at[hop - 1], val_r.at[isl]),
             {"island": (isl + hop) % islands})

    acc[...] = jnp.zeros_like(acc)

    def use(zo, xo, first, count):
        def body(i, carry):
            r = pl.multiple_of(first + i * 128, 128)
            cols = pl.ds(pl.multiple_of((zo * 2 + xo) * rows + r, 128), 128)
            block = wf[zo, xo, pl.ds(r, 128), :]
            acc[...] += jnp.dot(tok[:, cols], block, preferred_element_type=F32)
            tg_ref[:, cols] = lax.dot_general(
                cot_ref[...], block, (((1,), (1,)), ((), ())), preferred_element_type=F32
            ).astype(BF16)
            return carry

        lax.fori_loop(0, count // 128, body, 0)

    def use_a(zo, xo):
        use(zo, xo, 0, rows_a)

    def use_b(zo, xo):
        use(zo, xo, rows_a, rows - rows_a)

    def add(write, reads, count):
        def body(i, carry):
            here = pl.ds(pl.multiple_of(i * 64, 64), 64)
            total = reads[0][here, :].astype(F32)
            for ref in reads[1:]:
                total += ref[here, :].astype(F32)
            write(here, total)
            return carry

        lax.fori_loop(0, count // 64, body, 0)

    def into(ref):
        def write(here, total):
            ref[here, :] = total.astype(BF16)
        return write

    sb_start(0, True)
    sb_start(0, False)
    use(z, x, 0, rows)

    def gb_open():
        arrived(wf.at[z, ox, B], gbx.at[1])
        gb_send(z, x, True, True, own=True)
        gb_send(z, ox, True, True)

    rows_b = rows - rows_a

    for t in range(1, NZ):
        for zo, ok, up in ((z - t, z - t >= 0, True), (z + t, z + t < NZ, False)):
            @pl.when(ok)
            def _(zo=zo, ok=ok):
                arrived(wf.at[zo, x, A], ga_r.at[zo])
            if up:
                ga_send(zo, ok, False)
            else:
                ga_send(zo, False, ok)

        zt = NZ - 1 - t + z
        c = jnp.logical_and(has_dn, zt < NZ)
        go = jnp.logical_and(c, zt > z)

        @pl.when(go)
        def _(zt=zt, go=go):
            for xo in range(2):
                arrived(up_b.at[zt, xo], sb_up.at[zt, xo])
                add(into(part.at[zt, xo, B]), [part.at[zt, xo, B], up_b.at[zt, xo]], rows_b)
                sb_send(zt, xo, True, go)

        zd = t + z - (NZ - 1)
        c = jnp.logical_and(has_up, zd >= 0)
        gd = jnp.logical_and(c, zd < z)

        @pl.when(gd)
        def _(zd=zd, gd=gd):
            for xo in range(2):
                arrived(dn_b.at[zd, xo], sb_dn.at[zd, xo])
                add(into(part.at[zd, xo, B]), [part.at[zd, xo, B], dn_b.at[zd, xo]], rows_b)
                sb_send(zd, xo, False, gd)

        if t < NZ - 1:
            sb_start(t, True)
            sb_start(t, False)
        if t == NZ - 2:
            gb_open()
            arrived(xr_a.at[NZ - 1], sax_r.at[NZ - 1])
            gax_send(z, None)
        for zo, ok in ((z - t, z - t >= 0), (z + t, z + t < NZ)):
            @pl.when(ok)
            def _(zo=zo):
                use_a(zo, x)

    def b_sums(xo, write):
        own = part.at[z, xo, B]

        @pl.when(has_dn)
        def _():
            arrived(up_b.at[z, xo], sb_up.at[z, xo])

        @pl.when(has_up)
        def _():
            arrived(dn_b.at[z, xo], sb_dn.at[z, xo])

        @pl.when(jnp.logical_and(has_dn, has_up))
        def _():
            add(write, [own, up_b.at[z, xo], dn_b.at[z, xo]], rows_b)

        @pl.when(jnp.logical_not(has_dn))
        def _():
            add(write, [own, dn_b.at[z, xo]], rows_b)

        @pl.when(jnp.logical_not(has_up))
        def _():
            add(write, [own, up_b.at[z, xo]], rows_b)

    def wg_b(here, total):
        wg_ref[pl.ds(pl.multiple_of(rows_a + here.start, 64), 64), :] = total

    def sa_send(zt, up, cond, early=None):
        if up:
            send(lambda: (part.at[zt, x, A], up_a.at[zt], sa_s.at[zt], sa_up.at[zt]), above, cond,
                 early)
        else:
            send(lambda: (part.at[zt, x, A], dn_a.at[zt], sa_s.at[zt], sa_dn.at[zt]), below, cond,
                 early)

    def sa_start(t, up):
        zt = NZ - 1 - t if up else t
        c = first if up else last
        to = above if up else below

        @pl.when(c)
        def _():
            add(into(part.at[zt, x, A]), [part.at[zt, x, A], xr_a.at[zt]], rows_a)
            if t == 0:
                if up:
                    sent(lambda: (wf.at[z, x, B], wf.at[z, x, B], gb_up.at[z, x], gb_r.at[z, x]), to)
                else:
                    sent(lambda: (wf.at[z, x, B], wf.at[z, x, B], gb_dn.at[z, x], gb_r.at[z, x]), to)
            else:
                before = zt + 1 if up else zt - 1
                sent(lambda: (part.at[before, x, A], up_a.at[before], sa_s.at[before],
                              sa_up.at[before]), to)
            sa_send(zt, up, c, True if t < NZ - 2 else None)

    for zt, t in ((0, 1), (2, 2), (1, 3)):
        arrived(xr_a.at[zt], sax_r.at[zt])
        for zo, ok in ((z - t, z - t >= 0), (z + t, z + t < NZ)):
            @pl.when(ok)
            def _(zo=zo, ok=ok):
                gax_send(zo, ok)
    use_b(z, ox)
    sa_start(0, True)
    sa_start(0, False)

    b_sums(ox, into(part.at[z, ox, B]))
    send(lambda: (part.at[z, ox, B], xr_b, sbx.at[0], sbx.at[1]), flip)
    b_sums(x, wg_b)

    arrived(wf.at[z, ox, A], gax_r.at[z])
    use_a(z, ox)

    for hop in range(1, islands):
        other = (isl + hop) % islands
        arrived(vals.at[other], val_r.at[other])

    width = codes_ref.shape[1]

    def outer(i, carry):
        span = pl.ds(pl.multiple_of(i * 512, 512), 512)
        total = vals[0, :, span].astype(F32)
        for j in range(1, islands):
            total += vals[j, :, span].astype(F32)
        delta = total / islands
        new = 0.9 * mom_ref[:, span] + delta
        nmom_ref[:, span] = new
        npar_ref[:, span] = par_ref[:, span] - 0.7 * (delta + 0.9 * new)
        return carry

    lax.fori_loop(0, width // 512, outer, 0)

    for t in range(1, NZ):
        for zo, ok, up in ((z - t, z - t >= 0, True), (z + t, z + t < NZ, False)):
            for xo in range(2):
                @pl.when(ok)
                def _(zo=zo, xo=xo):
                    arrived(wf.at[zo, xo, B], gb_r.at[zo, xo])
                if up:
                    gb_send(zo, xo, ok, False)
                else:
                    gb_send(zo, xo, False, ok)

        zt = NZ - 1 - t + z
        go = jnp.logical_and(jnp.logical_and(has_dn, zt < NZ), zt > z)

        @pl.when(go)
        def _(zt=zt, go=go):
            arrived(up_a.at[zt], sa_up.at[zt])
            add(into(part.at[zt, x, A]), [part.at[zt, x, A], xr_a.at[zt], up_a.at[zt]], rows_a)
            sa_send(zt, True, go)

        zd = t + z - (NZ - 1)
        gd = jnp.logical_and(jnp.logical_and(has_up, zd >= 0), zd < z)

        @pl.when(gd)
        def _(zd=zd, gd=gd):
            arrived(dn_a.at[zd], sa_dn.at[zd])
            add(into(part.at[zd, x, A]), [part.at[zd, x, A], xr_a.at[zd], dn_a.at[zd]], rows_a)
            sa_send(zd, False, gd)

        if t < NZ - 1:
            sa_start(t, True)
            sa_start(t, False)

        for zo, ok in ((z - t, z - t >= 0), (z + t, z + t < NZ)):
            @pl.when(ok)
            def _(zo=zo):
                use_b(zo, 0)
                use_b(zo, 1)
                arrived(wf.at[zo, ox, A], gax_r.at[zo])
                use_a(zo, ox)

    proj_ref[...] = acc[...].astype(BF16)

    arrived(xr_b, sbx.at[1])

    def last_b(i, carry):
        here = pl.ds(pl.multiple_of(i * 64, 64), 64)
        there = pl.ds(pl.multiple_of(rows_a + i * 64, 64), 64)
        wg_ref[there, :] = (wg_ref[there, :] + xr_b[here, :].astype(F32)) * scaling
        return carry

    lax.fori_loop(0, rows_b // 64, last_b, 0)

    def wg_a(here, total):
        wg_ref[here, :] = total * scaling

    own = [part.at[z, x, A], xr_a.at[z]]

    @pl.when(has_dn)
    def _():
        arrived(up_a.at[z], sa_up.at[z])

    @pl.when(has_up)
    def _():
        arrived(dn_a.at[z], sa_dn.at[z])

    @pl.when(jnp.logical_and(has_dn, has_up))
    def _():
        add(wg_a, own + [up_a.at[z], dn_a.at[z]], rows_a)

    @pl.when(jnp.logical_not(has_dn))
    def _():
        add(wg_a, own + [dn_a.at[z]], rows_a)

    @pl.when(jnp.logical_not(has_up))
    def _():
        add(wg_a, own + [up_a.at[z]], rows_a)

    for cond, early, copy in pending:
        if early is not None:
            cond = jnp.logical_and(cond, jnp.logical_not(early))
        if cond is None:
            copy().wait_send()
        else:
            pl.when(cond)(lambda copy=copy: copy().wait_send())


def grid_local(
    islands,
    tokens, cotangent, key_weight, quant_codes, zero_points, minima, quant_steps, momentum, params
):
    tok_rows, width = tokens.shape[1:]
    rows, heads = key_weight.shape[1:]
    frag, groups = zero_points.shape[1:]
    rows_a = rows // 128 * 5 // 8 * 128
    rows_b = rows - rows_a
    scaling = 1.0 / math.sqrt(tok_rows * 2 * NZ)
    vmem = pl.BlockSpec(memory_space=pltpu.VMEM)
    hbm = pl.BlockSpec(memory_space=pltpu.HBM)
    dma = pltpu.SemaphoreType.DMA
    outs = pl.pallas_call(
        functools.partial(kernel, islands, rows_a, scaling),
        out_shape=(
            pltpu.VMEM((tok_rows, heads), BF16),
            pltpu.VMEM((tok_rows, width), BF16),
            pltpu.VMEM((rows, heads), F32),
            pltpu.VMEM((frag, width), F32),
            pltpu.VMEM((frag, width), F32),
        ),
        in_specs=[hbm] * 9,
        out_specs=[vmem] * 5,
        scratch_shapes=[
            pltpu.VMEM((tok_rows, width), BF16),
            pltpu.VMEM((tok_rows, heads), BF16),
            pltpu.VMEM((frag, width), jnp.int32),
            pltpu.VMEM((frag, groups), jnp.int32),
            pltpu.VMEM((frag, groups), F32),
            pltpu.VMEM((frag, groups), F32),
            pltpu.VMEM((frag, width), F32),
            pltpu.VMEM((frag, width), F32),
            pltpu.VMEM((NZ, 2, rows, heads), BF16),
            pltpu.VMEM((NZ, 2, rows, heads), BF16),
            pltpu.VMEM((NZ, rows_a, heads), BF16),
            pltpu.VMEM((NZ, rows_a, heads), BF16),
            pltpu.VMEM((NZ, rows_a, heads), BF16),
            pltpu.VMEM((NZ, 2, rows_b, heads), BF16),
            pltpu.VMEM((NZ, 2, rows_b, heads), BF16),
            pltpu.VMEM((rows_b, heads), BF16),
            pltpu.VMEM((islands, frag, width), BF16),
            pltpu.VMEM((tok_rows, heads), F32),
            dma((9,)),
            dma((NZ,)), dma((NZ,)), dma((NZ,)), dma((NZ,)), dma((NZ,)), dma((2,)),
            dma((NZ, 2)), dma((NZ, 2)), dma((NZ, 2)),
            dma((NZ,)), dma((NZ,)), dma((NZ,)), dma((NZ,)), dma((NZ,)),
            dma((NZ, 2)), dma((NZ, 2)), dma((NZ, 2)), dma((2,)),
            dma((islands - 1,)), dma((islands,)),
        ],
        compiler_params=pltpu.CompilerParams(
            collective_id=0, has_side_effects=True, vmem_limit_bytes=54 * 2**20
        ),
        cost_estimate=pl.CostEstimate(
            flops=6 * tok_rows * width * heads, bytes_accessed=20 * 2**20, transcendentals=0
        ),
    )(
        tokens[0], cotangent[0], key_weight[0], quant_codes[0], zero_points[0], minima[0],
        quant_steps[0], momentum, params,
    )
    projected, token_grad, weight_grad, new_momentum, new_params = outs
    return (projected[None], token_grad[None], weight_grad[None], new_momentum, new_params)


def solution(mesh):
    placed = (P("island", "fsdp", None),) * 7 + (P("fsdp", None),) * 2
    if mesh.shape["fsdp"] == 2 * NZ:
        body = functools.partial(grid_local, mesh.shape["island"])
    else:
        body = local
    return jax.shard_map(
        body,
        mesh=mesh,
        in_specs=placed,
        out_specs=(P("island", "fsdp", None),) * 3 + (P("fsdp", None),) * 2,
        check_vma=False,
    )
```

```python
import functools
import math

import jax
import jax.numpy as jnp
from jax import lax
from jax.experimental import pallas as pl
from jax.experimental.pallas import tpu as pltpu
from jax.sharding import PartitionSpec as P

GROUP = 128
MESH = pl.DeviceIdType.MESH
F32 = jnp.float32
BF16 = jnp.bfloat16
NZ = 4


def dequantize(quant_codes, zero_points, minima, quant_steps):
    shape = quant_codes.shape
    grouped = quant_codes.reshape(shape[:-1] + (shape[-1] // GROUP, GROUP))
    offset = (grouped - zero_points[..., None]).astype(F32)
    values = quant_steps[..., None] * offset + minima[..., None]
    return values.reshape(shape)


def local(
    tokens, cotangent, key_weight, quant_codes, zero_points, minima, quant_steps, momentum, params
):
    inputs = tokens[0]
    cot_rows = cotangent[0]
    weight = key_weight[0]
    island_tok = inputs.shape[0] * lax.axis_size("fsdp")
    scaling = 1.0 / math.sqrt(island_tok)
    piece = lax.all_gather(weight, "fsdp", axis=0, tiled=True)
    projected = jnp.dot(inputs, piece, preferred_element_type=F32).astype(BF16)
    back_acc = lax.dot_general(
        cot_rows, piece, (((1,), (1,)), ((), ())), preferred_element_type=F32
    ).astype(BF16)
    grad = lax.psum_scatter(
        lax.dot_general(inputs, cot_rows, (((0,), (0,)), ((), ())), preferred_element_type=F32),
        "fsdp",
        scatter_dimension=0,
        tiled=True,
    )
    weight_grad = grad * scaling
    values = dequantize(quant_codes[0], zero_points[0], minima[0], quant_steps[0])
    replicas = lax.axis_size("island")
    summed = lax.psum(values.astype(BF16), "island").astype(F32)
    delta = summed / replicas
    new_momentum = 0.9 * momentum + delta
    new_params = params - 0.7 * (delta + 0.9 * new_momentum)
    return (projected[None], back_acc[None], weight_grad[None], new_momentum, new_params)


def kernel(
    islands, rows_a, scaling,
    tok_hbm, cot_hbm, w_hbm, codes_hbm, zp_hbm, min_hbm, step_hbm, mom_hbm, par_hbm,
    proj_ref, tg_ref, wg_ref, nmom_ref, npar_ref,
    tok, cot_ref, codes_ref, zp_ref, min_ref, step_ref, mom_ref, par_ref, wf, part, xr_a, up_a, dn_a, up_b, dn_b, xr_b, vals, acc,
    in_sem, ga_up, ga_dn, ga_r, gax_s, gax_r, gbx, gb_up, gb_dn, gb_r,
    sax_s, sax_r, sa_s, sa_up, sa_dn, sb_s, sb_up, sb_dn, sbx, val_s, val_r,
):
    me = lax.axis_index("fsdp")
    isl = lax.axis_index("island")
    z, x = me // 2, me % 2
    ox = 1 - x
    rows = w_hbm.shape[0]
    A = pl.ds(0, rows_a)
    B = pl.ds(rows_a, rows - rows_a)
    flip = {"fsdp": me + 1 - 2 * x}
    above = {"fsdp": me + 2}
    below = {"fsdp": me - 2}
    has_up = z < NZ - 1
    has_dn = z > 0

    pending = []

    def send(make, to, cond=None, early=None):
        def copy():
            src, dst, ssem, rsem = make()
            return pltpu.make_async_remote_copy(
                src_ref=src, dst_ref=dst, send_sem=ssem, recv_sem=rsem,
                device_id=to, device_id_type=MESH)
        if early is not True:
            pending.append((cond, early, copy))
        copy().start()

    def arrived(dst, rsem):
        pltpu.make_async_remote_copy(
            src_ref=dst, dst_ref=dst, send_sem=rsem, recv_sem=rsem,
            device_id=flip, device_id_type=MESH).wait_recv()

    tok_in = pltpu.make_async_copy(tok_hbm, tok, in_sem.at[0])
    w_in = pltpu.make_async_copy(w_hbm, wf.at[z, x], in_sem.at[1])
    cot_in = pltpu.make_async_copy(cot_hbm, cot_ref, in_sem.at[2])
    quant_in = [
        pltpu.make_async_copy(src, dst, in_sem.at[3 + i])
        for i, (src, dst) in enumerate((
            (codes_hbm, codes_ref), (zp_hbm, zp_ref), (min_hbm, min_ref), (step_hbm, step_ref),
            (mom_hbm, mom_ref), (par_hbm, par_ref)))
    ]
    w_in.start()
    cot_in.start()
    tok_in.start()
    for copy in quant_in:
        copy.start()

    barrier = pltpu.get_barrier_semaphore()
    pl.semaphore_signal(barrier, inc=1, device_id=flip, device_id_type=MESH)

    @pl.when(has_up)
    def _():
        pl.semaphore_signal(barrier, inc=1, device_id=above, device_id_type=MESH)

    @pl.when(has_dn)
    def _():
        pl.semaphore_signal(barrier, inc=1, device_id=below, device_id_type=MESH)

    for hop in range(1, islands):
        pl.semaphore_signal(
            barrier, inc=1, device_id={"island": (isl + hop) % islands}, device_id_type=MESH)
    pl.semaphore_wait(barrier, islands + has_up.astype(jnp.int32) + has_dn.astype(jnp.int32))

    first, last = z == 0, z == NZ - 1

    def ga_send(zo, up, dn, own=False):
        c_up = jnp.logical_and(has_up, up)
        c_dn = jnp.logical_and(has_dn, dn)

        @pl.when(c_up)
        def _():
            send(lambda: (wf.at[zo, x, A], wf.at[zo, x, A], ga_up.at[zo], ga_r.at[zo]), above, c_up,
                 first if own else None)

        @pl.when(c_dn)
        def _():
            send(lambda: (wf.at[zo, x, A], wf.at[zo, x, A], ga_dn.at[zo], ga_r.at[zo]), below, c_dn,
                 last if own else None)

    def gax_send(zo, cond):
        send(lambda: (wf.at[zo, x, A], wf.at[zo, x, A], gax_s.at[zo], gax_r.at[zo]), flip, cond)

    def gb_send(zo, xo, up, dn, own=False):
        c_up = jnp.logical_and(has_up, up)
        c_dn = jnp.logical_and(has_dn, dn)

        @pl.when(c_up)
        def _():
            send(lambda: (wf.at[zo, xo, B], wf.at[zo, xo, B], gb_up.at[zo, xo], gb_r.at[zo, xo]),
                 above, c_up, first if own else None)

        @pl.when(c_dn)
        def _():
            send(lambda: (wf.at[zo, xo, B], wf.at[zo, xo, B], gb_dn.at[zo, xo], gb_r.at[zo, xo]),
                 below, c_dn, last if own else None)

    w_in.wait()
    send(lambda: (wf.at[z, x, B], wf.at[z, x, B], gbx.at[0], gbx.at[1]), flip)
    ga_send(z, True, True, own=True)

    cot_in.wait()
    tok_in.wait()
    cot = cot_ref[...]

    def sb_send(zt, xo, up, cond, early=None):
        if up:
            send(lambda: (part.at[zt, xo, B], up_b.at[zt, xo], sb_s.at[zt, xo], sb_up.at[zt, xo]),
                 above, cond, early)
        else:
            send(lambda: (part.at[zt, xo, B], dn_b.at[zt, xo], sb_s.at[zt, xo], sb_dn.at[zt, xo]),
                 below, cond, early)

    def sent(make, to):
        src, dst, ssem, rsem = make()
        pltpu.make_async_remote_copy(
            src_ref=src, dst_ref=dst, send_sem=ssem, recv_sem=rsem,
            device_id=to, device_id_type=MESH).wait_send()

    def sb_start(t, up):
        end = 0 if up else NZ - 1
        zt = NZ - 1 - t if up else t
        c = z == end
        to = above if up else below

        @pl.when(c)
        def _():
            if t == 0:
                if up:
                    sent(lambda: (wf.at[z, x, A], wf.at[z, x, A], ga_up.at[z], ga_r.at[z]), to)
                else:
                    sent(lambda: (wf.at[z, x, A], wf.at[z, x, A], ga_dn.at[z], ga_r.at[z]), to)
            else:
                before = zt + 1 if up else zt - 1
                sent(lambda: (part.at[before, 0, B], up_b.at[before, 0], sb_s.at[before, 0],
                              sb_up.at[before, 0]), to)
            for xo in range(2):
                sb_send(zt, xo, up, c, True if xo == 0 and t < NZ - 2 else None)

    tile = 256
    tiles = rows // tile
    for zt in (NZ - 1, 0, 2, 1):
        def grad_tile(i, carry, zt=zt):
            xo, r = i // tiles, (i % tiles) * tile
            cols = pl.ds(pl.multiple_of((zt * 2 + xo) * rows + r, tile), tile)
            part[zt, xo, pl.ds(pl.multiple_of(r, tile), tile), :] = lax.dot_general(
                tok[:, cols], cot, (((0,), (0,)), ((), ())), preferred_element_type=F32
            ).astype(BF16)
            return carry

        lax.fori_loop(0, 2 * tiles, grad_tile, 0)
        send(lambda zt=zt: (part.at[zt, ox, A], xr_a.at[zt], sax_s.at[zt], sax_r.at[zt]), flip)

    for copy in quant_in:
        copy.wait()

    for g in range(zp_ref.shape[1]):
        span = slice(g * GROUP, (g + 1) * GROUP)
        one = slice(g, g + 1)
        offset = (codes_ref[:, span] - zp_ref[:, one]).astype(F32)
        vals[isl, :, span] = (step_ref[:, one] * offset + min_ref[:, one]).astype(BF16)
    for hop in range(1, islands):
        send(lambda hop=hop: (vals.at[isl], vals.at[isl], val_s.at[hop - 1], val_r.at[isl]),
             {"island": (isl + hop) % islands})

    acc[...] = jnp.zeros_like(acc)

    def use(zo, xo, first, count):
        def body(i, carry):
            r = pl.multiple_of(first + i * 128, 128)
            cols = pl.ds(pl.multiple_of((zo * 2 + xo) * rows + r, 128), 128)
            block = wf[zo, xo, pl.ds(r, 128), :]
            acc[...] += jnp.dot(tok[:, cols], block, preferred_element_type=F32)
            tg_ref[:, cols] = lax.dot_general(
                cot_ref[...], block, (((1,), (1,)), ((), ())), preferred_element_type=F32
            ).astype(BF16)
            return carry

        lax.fori_loop(0, count // 128, body, 0)

    half = rows // 2

    def use_a(zo, xo):
        use(zo, xo, 0, half)

    def use_b(zo, xo):
        use(zo, xo, half, rows - half)

    def add(write, reads, count):
        def body(i, carry):
            here = pl.ds(pl.multiple_of(i * 32, 32), 32)
            total = reads[0][here, :].astype(F32)
            for ref in reads[1:]:
                total += ref[here, :].astype(F32)
            write(here, total)
            return carry

        lax.fori_loop(0, count // 32, body, 0)

    def into(ref):
        def write(here, total):
            ref[here, :] = total.astype(BF16)
        return write

    sb_start(0, True)
    sb_start(0, False)
    use(z, x, 0, rows)

    def gb_open():
        arrived(wf.at[z, ox, B], gbx.at[1])
        gb_send(z, x, True, True, own=True)
        gb_send(z, ox, True, True)

    rows_b = rows - rows_a

    for t in range(1, NZ):
        for zo, ok, up in ((z - t, z - t >= 0, True), (z + t, z + t < NZ, False)):
            @pl.when(ok)
            def _(zo=zo, ok=ok):
                arrived(wf.at[zo, x, A], ga_r.at[zo])
            if up:
                ga_send(zo, ok, False)
            else:
                ga_send(zo, False, ok)

        zt = NZ - 1 - t + z
        c = jnp.logical_and(has_dn, zt < NZ)
        go = jnp.logical_and(c, zt > z)

        @pl.when(go)
        def _(zt=zt, go=go):
            for xo in range(2):
                arrived(up_b.at[zt, xo], sb_up.at[zt, xo])
                add(into(part.at[zt, xo, B]), [part.at[zt, xo, B], up_b.at[zt, xo]], rows_b)
                sb_send(zt, xo, True, go)

        zd = t + z - (NZ - 1)
        c = jnp.logical_and(has_up, zd >= 0)
        gd = jnp.logical_and(c, zd < z)

        @pl.when(gd)
        def _(zd=zd, gd=gd):
            for xo in range(2):
                arrived(dn_b.at[zd, xo], sb_dn.at[zd, xo])
                add(into(part.at[zd, xo, B]), [part.at[zd, xo, B], dn_b.at[zd, xo]], rows_b)
                sb_send(zd, xo, False, gd)

        if t < NZ - 1:
            sb_start(t, True)
            sb_start(t, False)
        if t == NZ - 2:
            gb_open()
            arrived(xr_a.at[NZ - 1], sax_r.at[NZ - 1])
            gax_send(z, None)
        for zo, ok in ((z - t, z - t >= 0), (z + t, z + t < NZ)):
            @pl.when(ok)
            def _(zo=zo):
                use_a(zo, x)

    def b_sums(xo, write):
        own = part.at[z, xo, B]

        @pl.when(has_dn)
        def _():
            arrived(up_b.at[z, xo], sb_up.at[z, xo])

        @pl.when(has_up)
        def _():
            arrived(dn_b.at[z, xo], sb_dn.at[z, xo])

        @pl.when(jnp.logical_and(has_dn, has_up))
        def _():
            add(write, [own, up_b.at[z, xo], dn_b.at[z, xo]], rows_b)

        @pl.when(jnp.logical_not(has_dn))
        def _():
            add(write, [own, dn_b.at[z, xo]], rows_b)

        @pl.when(jnp.logical_not(has_up))
        def _():
            add(write, [own, up_b.at[z, xo]], rows_b)

    def wg_b(here, total):
        wg_ref[pl.ds(pl.multiple_of(rows_a + here.start, 32), 32), :] = total

    def sa_send(zt, up, cond, early=None):
        if up:
            send(lambda: (part.at[zt, x, A], up_a.at[zt], sa_s.at[zt], sa_up.at[zt]), above, cond,
                 early)
        else:
            send(lambda: (part.at[zt, x, A], dn_a.at[zt], sa_s.at[zt], sa_dn.at[zt]), below, cond,
                 early)

    def sa_start(t, up):
        zt = NZ - 1 - t if up else t
        c = first if up else last
        to = above if up else below

        @pl.when(c)
        def _():
            add(into(part.at[zt, x, A]), [part.at[zt, x, A], xr_a.at[zt]], rows_a)
            if t == 0:
                if up:
                    sent(lambda: (wf.at[z, x, B], wf.at[z, x, B], gb_up.at[z, x], gb_r.at[z, x]), to)
                else:
                    sent(lambda: (wf.at[z, x, B], wf.at[z, x, B], gb_dn.at[z, x], gb_r.at[z, x]), to)
            else:
                before = zt + 1 if up else zt - 1
                sent(lambda: (part.at[before, x, A], up_a.at[before], sa_s.at[before],
                              sa_up.at[before]), to)
            sa_send(zt, up, c, True if t < NZ - 2 else None)

    for zt, t in ((0, 1), (2, 2), (1, 3)):
        arrived(xr_a.at[zt], sax_r.at[zt])
        for zo, ok in ((z - t, z - t >= 0), (z + t, z + t < NZ)):
            @pl.when(ok)
            def _(zo=zo, ok=ok):
                gax_send(zo, ok)
    sa_start(0, True)
    sa_start(0, False)

    b_sums(ox, into(part.at[z, ox, B]))
    send(lambda: (part.at[z, ox, B], xr_b, sbx.at[0], sbx.at[1]), flip)
    b_sums(x, wg_b)

    arrived(wf.at[z, ox, A], gax_r.at[z])
    use(z, ox, 0, rows)

    for hop in range(1, islands):
        other = (isl + hop) % islands
        arrived(vals.at[other], val_r.at[other])

    width = codes_ref.shape[1]

    def outer(i, carry):
        span = pl.ds(pl.multiple_of(i * 512, 512), 512)
        total = vals[0, :, span].astype(F32)
        for j in range(1, islands):
            total += vals[j, :, span].astype(F32)
        delta = total / islands
        new = 0.9 * mom_ref[:, span] + delta
        nmom_ref[:, span] = new
        npar_ref[:, span] = par_ref[:, span] - 0.7 * (delta + 0.9 * new)
        return carry

    lax.fori_loop(0, width // 512, outer, 0)

    for t in range(1, NZ):
        for zo, ok, up in ((z - t, z - t >= 0, True), (z + t, z + t < NZ, False)):
            for xo in range(2):
                @pl.when(ok)
                def _(zo=zo, xo=xo):
                    arrived(wf.at[zo, xo, B], gb_r.at[zo, xo])
                if up:
                    gb_send(zo, xo, ok, False)
                else:
                    gb_send(zo, xo, False, ok)

        zt = NZ - 1 - t + z
        go = jnp.logical_and(jnp.logical_and(has_dn, zt < NZ), zt > z)

        @pl.when(go)
        def _(zt=zt, go=go):
            arrived(up_a.at[zt], sa_up.at[zt])
            add(into(part.at[zt, x, A]), [part.at[zt, x, A], xr_a.at[zt], up_a.at[zt]], rows_a)
            sa_send(zt, True, go)

        zd = t + z - (NZ - 1)
        gd = jnp.logical_and(jnp.logical_and(has_up, zd >= 0), zd < z)

        @pl.when(gd)
        def _(zd=zd, gd=gd):
            arrived(dn_a.at[zd], sa_dn.at[zd])
            add(into(part.at[zd, x, A]), [part.at[zd, x, A], xr_a.at[zd], dn_a.at[zd]], rows_a)
            sa_send(zd, False, gd)

        if t < NZ - 1:
            sa_start(t, True)
            sa_start(t, False)

        for zo, ok in ((z - t, z - t >= 0), (z + t, z + t < NZ)):
            @pl.when(ok)
            def _(zo=zo):
                use_b(zo, x)
                arrived(wf.at[zo, ox, A], gax_r.at[zo])
                use(zo, ox, 0, rows)

    proj_ref[...] = acc[...].astype(BF16)

    arrived(xr_b, sbx.at[1])

    def last_b(i, carry):
        here = pl.ds(pl.multiple_of(i * 32, 32), 32)
        there = pl.ds(pl.multiple_of(rows_a + i * 32, 32), 32)
        wg_ref[there, :] = (wg_ref[there, :] + xr_b[here, :].astype(F32)) * scaling
        return carry

    lax.fori_loop(0, rows_b // 32, last_b, 0)

    def wg_a(here, total):
        wg_ref[here, :] = total * scaling

    own = [part.at[z, x, A], xr_a.at[z]]

    @pl.when(has_dn)
    def _():
        arrived(up_a.at[z], sa_up.at[z])

    @pl.when(has_up)
    def _():
        arrived(dn_a.at[z], sa_dn.at[z])

    @pl.when(jnp.logical_and(has_dn, has_up))
    def _():
        add(wg_a, own + [up_a.at[z], dn_a.at[z]], rows_a)

    @pl.when(jnp.logical_not(has_dn))
    def _():
        add(wg_a, own + [dn_a.at[z]], rows_a)

    @pl.when(jnp.logical_not(has_up))
    def _():
        add(wg_a, own + [up_a.at[z]], rows_a)

    for cond, early, copy in pending:
        if early is not None:
            cond = jnp.logical_and(cond, jnp.logical_not(early))
        if cond is None:
            copy().wait_send()
        else:
            pl.when(cond)(lambda copy=copy: copy().wait_send())


def write_out(*refs):
    n = len(refs) // 2
    copies = [pltpu.make_async_copy(refs[i], refs[n + i], refs[-1].at[i]) for i in range(n)]
    for copy in copies:
        copy.start()
    for copy in copies:
        copy.wait()


def grid_local(
    islands,
    tokens, cotangent, key_weight, quant_codes, zero_points, minima, quant_steps, momentum, params
):
    tok_rows, width = tokens.shape[1:]
    rows, heads = key_weight.shape[1:]
    frag, groups = zero_points.shape[1:]
    rows_a = rows * 3 // 5 // 32 * 32
    rows_b = rows - rows_a
    scaling = 1.0 / math.sqrt(tok_rows * 2 * NZ)
    vmem = pl.BlockSpec(memory_space=pltpu.VMEM)
    hbm = pl.BlockSpec(memory_space=pltpu.HBM)
    dma = pltpu.SemaphoreType.DMA
    outs = pl.pallas_call(
        functools.partial(kernel, islands, rows_a, scaling),
        out_shape=(
            pltpu.VMEM((tok_rows, heads), BF16),
            pltpu.VMEM((tok_rows, width), BF16),
            pltpu.VMEM((rows, heads), F32),
            pltpu.VMEM((frag, width), F32),
            pltpu.VMEM((frag, width), F32),
        ),
        in_specs=[hbm] * 9,
        out_specs=[vmem] * 5,
        scratch_shapes=[
            pltpu.VMEM((tok_rows, width), BF16),
            pltpu.VMEM((tok_rows, heads), BF16),
            pltpu.VMEM((frag, width), jnp.int32),
            pltpu.VMEM((frag, groups), jnp.int32),
            pltpu.VMEM((frag, groups), F32),
            pltpu.VMEM((frag, groups), F32),
            pltpu.VMEM((frag, width), F32),
            pltpu.VMEM((frag, width), F32),
            pltpu.VMEM((NZ, 2, rows, heads), BF16),
            pltpu.VMEM((NZ, 2, rows, heads), BF16),
            pltpu.VMEM((NZ, rows_a, heads), BF16),
            pltpu.VMEM((NZ, rows_a, heads), BF16),
            pltpu.VMEM((NZ, rows_a, heads), BF16),
            pltpu.VMEM((NZ, 2, rows_b, heads), BF16),
            pltpu.VMEM((NZ, 2, rows_b, heads), BF16),
            pltpu.VMEM((rows_b, heads), BF16),
            pltpu.VMEM((islands, frag, width), BF16),
            pltpu.VMEM((tok_rows, heads), F32),
            dma((9,)),
            dma((NZ,)), dma((NZ,)), dma((NZ,)), dma((NZ,)), dma((NZ,)), dma((2,)),
            dma((NZ, 2)), dma((NZ, 2)), dma((NZ, 2)),
            dma((NZ,)), dma((NZ,)), dma((NZ,)), dma((NZ,)), dma((NZ,)),
            dma((NZ, 2)), dma((NZ, 2)), dma((NZ, 2)), dma((2,)),
            dma((islands - 1,)), dma((islands,)),
        ],
        compiler_params=pltpu.CompilerParams(
            collective_id=0, has_side_effects=True, vmem_limit_bytes=54 * 2**20
        ),
        cost_estimate=pl.CostEstimate(
            flops=6 * tok_rows * width * heads, bytes_accessed=20 * 2**20, transcendentals=0
        ),
    )(
        tokens[0], cotangent[0], key_weight[0], quant_codes[0], zero_points[0], minima[0],
        quant_steps[0], momentum, params,
    )
    projected, token_grad, weight_grad, new_momentum, new_params = pl.pallas_call(
        write_out,
        out_shape=tuple(jax.ShapeDtypeStruct(out.shape, out.dtype) for out in outs),
        in_specs=[pl.BlockSpec(memory_space=pl.ANY)] * len(outs),
        out_specs=[hbm] * len(outs),
        scratch_shapes=[dma((len(outs),))],
        cost_estimate=pl.CostEstimate(flops=0, bytes_accessed=8 * 2**20, transcendentals=0),
    )(*outs)
    return (projected[None], token_grad[None], weight_grad[None], new_momentum, new_params)


def solution(mesh):
    placed = (P("island", "fsdp", None),) * 7 + (P("fsdp", None),) * 2
    if mesh.shape["fsdp"] == 2 * NZ:
        body = functools.partial(grid_local, mesh.shape["island"])
    else:
        body = local
    return jax.shard_map(
        body,
        mesh=mesh,
        in_specs=placed,
        out_specs=(P("island", "fsdp", None),) * 3 + (P("fsdp", None),) * 2,
        check_vma=False,
    )
```

```python
import functools
import math

import jax
import jax.numpy as jnp
from jax import lax
from jax.experimental import pallas as pl
from jax.experimental.pallas import tpu as pltpu
from jax.sharding import PartitionSpec as P

GROUP = 128
MESH = pl.DeviceIdType.MESH
F32 = jnp.float32
BF16 = jnp.bfloat16
NZ = 4


def dequantize(quant_codes, zero_points, minima, quant_steps):
    shape = quant_codes.shape
    grouped = quant_codes.reshape(shape[:-1] + (shape[-1] // GROUP, GROUP))
    offset = (grouped - zero_points[..., None]).astype(F32)
    values = quant_steps[..., None] * offset + minima[..., None]
    return values.reshape(shape)


def local(
    tokens, cotangent, key_weight, quant_codes, zero_points, minima, quant_steps, momentum, params
):
    inputs = tokens[0]
    cot_rows = cotangent[0]
    weight = key_weight[0]
    island_tok = inputs.shape[0] * lax.axis_size("fsdp")
    scaling = 1.0 / math.sqrt(island_tok)
    piece = lax.all_gather(weight, "fsdp", axis=0, tiled=True)
    projected = jnp.dot(inputs, piece, preferred_element_type=F32).astype(BF16)
    back_acc = lax.dot_general(
        cot_rows, piece, (((1,), (1,)), ((), ())), preferred_element_type=F32
    ).astype(BF16)
    grad = lax.psum_scatter(
        lax.dot_general(inputs, cot_rows, (((0,), (0,)), ((), ())), preferred_element_type=F32),
        "fsdp",
        scatter_dimension=0,
        tiled=True,
    )
    weight_grad = grad * scaling
    values = dequantize(quant_codes[0], zero_points[0], minima[0], quant_steps[0])
    replicas = lax.axis_size("island")
    summed = lax.psum(values.astype(BF16), "island").astype(F32)
    delta = summed / replicas
    new_momentum = 0.9 * momentum + delta
    new_params = params - 0.7 * (delta + 0.9 * new_momentum)
    return (projected[None], back_acc[None], weight_grad[None], new_momentum, new_params)


def kernel(
    islands, rows_a, scaling,
    tok_hbm, cot_hbm, w_hbm, codes_hbm, zp_hbm, min_hbm, step_hbm, mom_hbm, par_hbm,
    proj_ref, tg_ref, wg_ref, nmom_ref, npar_ref,
    tok, cot_ref, codes_ref, zp_ref, min_ref, step_ref, mom_ref, par_ref, wf, part, xr_a, up_a, dn_a, up_b, dn_b, xr_b, vals, acc,
    in_sem, ga_up, ga_dn, ga_r, gax_s, gax_r, gbx, gb_up, gb_dn, gb_r,
    sax_s, sax_r, sa_s, sa_up, sa_dn, sb_s, sb_up, sb_dn, sbx, val_s, val_r,
):
    me = lax.axis_index("fsdp")
    isl = lax.axis_index("island")
    z, x = me // 2, me % 2
    ox = 1 - x
    rows = w_hbm.shape[0]
    A = pl.ds(0, rows_a)
    B = pl.ds(rows_a, rows - rows_a)
    flip = {"fsdp": me + 1 - 2 * x}
    above = {"fsdp": me + 2}
    below = {"fsdp": me - 2}
    has_up = z < NZ - 1
    has_dn = z > 0

    pending = []

    def send(make, to, cond=None, early=None):
        def copy():
            src, dst, ssem, rsem = make()
            return pltpu.make_async_remote_copy(
                src_ref=src, dst_ref=dst, send_sem=ssem, recv_sem=rsem,
                device_id=to, device_id_type=MESH)
        if early is not True:
            pending.append((cond, early, copy))
        copy().start()

    def arrived(dst, rsem):
        pltpu.make_async_remote_copy(
            src_ref=dst, dst_ref=dst, send_sem=rsem, recv_sem=rsem,
            device_id=flip, device_id_type=MESH).wait_recv()

    tok_in = pltpu.make_async_copy(tok_hbm, tok, in_sem.at[0])
    w_in = pltpu.make_async_copy(w_hbm, wf.at[z, x], in_sem.at[1])
    cot_in = pltpu.make_async_copy(cot_hbm, cot_ref, in_sem.at[2])
    quant_in = [
        pltpu.make_async_copy(src, dst, in_sem.at[3 + i])
        for i, (src, dst) in enumerate((
            (codes_hbm, codes_ref), (zp_hbm, zp_ref), (min_hbm, min_ref), (step_hbm, step_ref),
            (mom_hbm, mom_ref), (par_hbm, par_ref)))
    ]
    w_in.start()
    cot_in.start()
    tok_in.start()
    for copy in quant_in:
        copy.start()

    barrier = pltpu.get_barrier_semaphore()
    pl.semaphore_signal(barrier, inc=1, device_id=flip, device_id_type=MESH)

    @pl.when(has_up)
    def _():
        pl.semaphore_signal(barrier, inc=1, device_id=above, device_id_type=MESH)

    @pl.when(has_dn)
    def _():
        pl.semaphore_signal(barrier, inc=1, device_id=below, device_id_type=MESH)

    for hop in range(1, islands):
        pl.semaphore_signal(
            barrier, inc=1, device_id={"island": (isl + hop) % islands}, device_id_type=MESH)
    pl.semaphore_wait(barrier, islands + has_up.astype(jnp.int32) + has_dn.astype(jnp.int32))

    first, last = z == 0, z == NZ - 1

    def ga_send(zo, up, dn, own=False):
        c_up = jnp.logical_and(has_up, up)
        c_dn = jnp.logical_and(has_dn, dn)

        @pl.when(c_up)
        def _():
            send(lambda: (wf.at[zo, x, A], wf.at[zo, x, A], ga_up.at[zo], ga_r.at[zo]), above, c_up,
                 first if own else None)

        @pl.when(c_dn)
        def _():
            send(lambda: (wf.at[zo, x, A], wf.at[zo, x, A], ga_dn.at[zo], ga_r.at[zo]), below, c_dn,
                 last if own else None)

    def gax_send(zo, cond):
        send(lambda: (wf.at[zo, x, A], wf.at[zo, x, A], gax_s.at[zo], gax_r.at[zo]), flip, cond)

    def gb_send(zo, xo, up, dn, own=False):
        c_up = jnp.logical_and(has_up, up)
        c_dn = jnp.logical_and(has_dn, dn)

        @pl.when(c_up)
        def _():
            send(lambda: (wf.at[zo, xo, B], wf.at[zo, xo, B], gb_up.at[zo, xo], gb_r.at[zo, xo]),
                 above, c_up, first if own else None)

        @pl.when(c_dn)
        def _():
            send(lambda: (wf.at[zo, xo, B], wf.at[zo, xo, B], gb_dn.at[zo, xo], gb_r.at[zo, xo]),
                 below, c_dn, last if own else None)

    w_in.wait()
    send(lambda: (wf.at[z, x, B], wf.at[z, x, B], gbx.at[0], gbx.at[1]), flip)
    ga_send(z, True, True, own=True)

    cot_in.wait()
    tok_in.wait()
    cot = cot_ref[...]

    def sb_send(zt, xo, up, cond, early=None):
        if up:
            send(lambda: (part.at[zt, xo, B], up_b.at[zt, xo], sb_s.at[zt, xo], sb_up.at[zt, xo]),
                 above, cond, early)
        else:
            send(lambda: (part.at[zt, xo, B], dn_b.at[zt, xo], sb_s.at[zt, xo], sb_dn.at[zt, xo]),
                 below, cond, early)

    def sent(make, to):
        src, dst, ssem, rsem = make()
        pltpu.make_async_remote_copy(
            src_ref=src, dst_ref=dst, send_sem=ssem, recv_sem=rsem,
            device_id=to, device_id_type=MESH).wait_send()

    def sb_start(t, up):
        end = 0 if up else NZ - 1
        zt = NZ - 1 - t if up else t
        c = z == end
        to = above if up else below

        @pl.when(c)
        def _():
            if t == 0:
                if up:
                    sent(lambda: (wf.at[z, x, A], wf.at[z, x, A], ga_up.at[z], ga_r.at[z]), to)
                else:
                    sent(lambda: (wf.at[z, x, A], wf.at[z, x, A], ga_dn.at[z], ga_r.at[z]), to)
            else:
                before = zt + 1 if up else zt - 1
                sent(lambda: (part.at[before, 0, B], up_b.at[before, 0], sb_s.at[before, 0],
                              sb_up.at[before, 0]), to)
            for xo in range(2):
                sb_send(zt, xo, up, c, True if xo == 0 and t < NZ - 2 else None)

    tile = 256
    tiles = rows // tile
    for zt in (NZ - 1, 0, 2, 1):
        def grad_tile(i, carry, zt=zt):
            xo, r = i // tiles, (i % tiles) * tile
            cols = pl.ds(pl.multiple_of((zt * 2 + xo) * rows + r, tile), tile)
            part[zt, xo, pl.ds(pl.multiple_of(r, tile), tile), :] = lax.dot_general(
                tok[:, cols], cot, (((0,), (0,)), ((), ())), preferred_element_type=F32
            ).astype(BF16)
            return carry

        lax.fori_loop(0, 2 * tiles, grad_tile, 0)
        send(lambda zt=zt: (part.at[zt, ox, A], xr_a.at[zt], sax_s.at[zt], sax_r.at[zt]), flip)

    sb_start(0, True)
    sb_start(0, False)

    def gather_a(t):
        for zo, ok, up in ((z - t, z - t >= 0, True), (z + t, z + t < NZ, False)):
            @pl.when(ok)
            def _(zo=zo):
                arrived(wf.at[zo, x, A], ga_r.at[zo])
            if up:
                ga_send(zo, ok, False)
            else:
                ga_send(zo, False, ok)

    gather_a(1)
    for copy in quant_in:
        copy.wait()

    for g in range(zp_ref.shape[1]):
        span = slice(g * GROUP, (g + 1) * GROUP)
        one = slice(g, g + 1)
        offset = (codes_ref[:, span] - zp_ref[:, one]).astype(F32)
        vals[isl, :, span] = (step_ref[:, one] * offset + min_ref[:, one]).astype(BF16)
    for hop in range(1, islands):
        send(lambda hop=hop: (vals.at[isl], vals.at[isl], val_s.at[hop - 1], val_r.at[isl]),
             {"island": (isl + hop) % islands})

    acc[...] = jnp.zeros_like(acc)

    def use(zo, xo, first, count):
        def body(i, carry):
            r = pl.multiple_of(first + i * 128, 128)
            cols = pl.ds(pl.multiple_of((zo * 2 + xo) * rows + r, 128), 128)
            block = wf[zo, xo, pl.ds(r, 128), :]
            acc[...] += jnp.dot(tok[:, cols], block, preferred_element_type=F32)
            tg_ref[:, cols] = lax.dot_general(
                cot_ref[...], block, (((1,), (1,)), ((), ())), preferred_element_type=F32
            ).astype(BF16)
            return carry

        lax.fori_loop(0, count // 128, body, 0)

    half = rows // 2

    def use_a(zo, xo):
        use(zo, xo, 0, half)

    def use_b(zo, xo):
        use(zo, xo, half, rows - half)

    def add(write, reads, count):
        def body(i, carry):
            here = pl.ds(pl.multiple_of(i * 32, 32), 32)
            total = reads[0][here, :].astype(F32)
            for ref in reads[1:]:
                total += ref[here, :].astype(F32)
            write(here, total)
            return carry

        lax.fori_loop(0, count // 32, body, 0)

    def into(ref):
        def write(here, total):
            ref[here, :] = total.astype(BF16)
        return write

    use(z, x, 0, rows)

    def gb_open():
        arrived(wf.at[z, ox, B], gbx.at[1])
        gb_send(z, x, True, True, own=True)
        gb_send(z, ox, True, True)

    rows_b = rows - rows_a

    gather_a(2)
    for t in range(1, NZ - 1):
        zt = NZ - 1 - t + z
        c = jnp.logical_and(has_dn, zt < NZ)
        go = jnp.logical_and(c, zt > z)

        @pl.when(go)
        def _(zt=zt, go=go):
            for xo in range(2):
                arrived(up_b.at[zt, xo], sb_up.at[zt, xo])
                add(into(part.at[zt, xo, B]), [part.at[zt, xo, B], up_b.at[zt, xo]], rows_b)
                sb_send(zt, xo, True, go)

        zd = t + z - (NZ - 1)
        c = jnp.logical_and(has_up, zd >= 0)
        gd = jnp.logical_and(c, zd < z)

        @pl.when(gd)
        def _(zd=zd, gd=gd):
            for xo in range(2):
                arrived(dn_b.at[zd, xo], sb_dn.at[zd, xo])
                add(into(part.at[zd, xo, B]), [part.at[zd, xo, B], dn_b.at[zd, xo]], rows_b)
                sb_send(zd, xo, False, gd)

        sb_start(t, True)
        sb_start(t, False)
        if t == NZ - 2:
            gb_open()
            arrived(xr_a.at[NZ - 1], sax_r.at[NZ - 1])
            gax_send(z, None)
        for zo, ok in ((z - t, z - t >= 0), (z + t, z + t < NZ)):
            @pl.when(ok)
            def _(zo=zo):
                use_a(zo, x)

    gather_a(NZ - 1)

    def b_sums(xo, write):
        own = part.at[z, xo, B]

        @pl.when(has_dn)
        def _():
            arrived(up_b.at[z, xo], sb_up.at[z, xo])

        @pl.when(has_up)
        def _():
            arrived(dn_b.at[z, xo], sb_dn.at[z, xo])

        @pl.when(jnp.logical_and(has_dn, has_up))
        def _():
            add(write, [own, up_b.at[z, xo], dn_b.at[z, xo]], rows_b)

        @pl.when(jnp.logical_not(has_dn))
        def _():
            add(write, [own, dn_b.at[z, xo]], rows_b)

        @pl.when(jnp.logical_not(has_up))
        def _():
            add(write, [own, up_b.at[z, xo]], rows_b)

    for zo, ok in ((z - NZ + 1, z - NZ + 1 >= 0), (z + NZ - 1, z + NZ - 1 < NZ)):
        @pl.when(ok)
        def _(zo=zo):
            use_a(zo, x)

    def wg_b(here, total):
        wg_ref[pl.ds(pl.multiple_of(rows_a + here.start, 32), 32), :] = total

    def sa_send(zt, up, cond, early=None):
        if up:
            send(lambda: (part.at[zt, x, A], up_a.at[zt], sa_s.at[zt], sa_up.at[zt]), above, cond,
                 early)
        else:
            send(lambda: (part.at[zt, x, A], dn_a.at[zt], sa_s.at[zt], sa_dn.at[zt]), below, cond,
                 early)

    def sa_start(t, up):
        zt = NZ - 1 - t if up else t
        c = first if up else last
        to = above if up else below

        @pl.when(c)
        def _():
            add(into(part.at[zt, x, A]), [part.at[zt, x, A], xr_a.at[zt]], rows_a)
            if t == 0:
                if up:
                    sent(lambda: (wf.at[z, x, B], wf.at[z, x, B], gb_up.at[z, x], gb_r.at[z, x]), to)
                else:
                    sent(lambda: (wf.at[z, x, B], wf.at[z, x, B], gb_dn.at[z, x], gb_r.at[z, x]), to)
            else:
                before = zt + 1 if up else zt - 1
                sent(lambda: (part.at[before, x, A], up_a.at[before], sa_s.at[before],
                              sa_up.at[before]), to)
            sa_send(zt, up, c, True if t < NZ - 2 else None)

    for zt, t in ((0, 1), (2, 2), (1, 3)):
        arrived(xr_a.at[zt], sax_r.at[zt])
        for zo, ok in ((z - t, z - t >= 0), (z + t, z + t < NZ)):
            @pl.when(ok)
            def _(zo=zo, ok=ok):
                gax_send(zo, ok)
    sa_start(0, True)
    sa_start(0, False)

    b_sums(ox, into(part.at[z, ox, B]))
    send(lambda: (part.at[z, ox, B], xr_b, sbx.at[0], sbx.at[1]), flip)
    b_sums(x, wg_b)

    arrived(wf.at[z, ox, A], gax_r.at[z])
    use(z, ox, 0, rows)

    for hop in range(1, islands):
        other = (isl + hop) % islands
        arrived(vals.at[other], val_r.at[other])

    width = codes_ref.shape[1]

    def outer(i, carry):
        span = pl.ds(pl.multiple_of(i * 512, 512), 512)
        total = vals[0, :, span].astype(F32)
        for j in range(1, islands):
            total += vals[j, :, span].astype(F32)
        delta = total / islands
        new = 0.9 * mom_ref[:, span] + delta
        nmom_ref[:, span] = new
        npar_ref[:, span] = par_ref[:, span] - 0.7 * (delta + 0.9 * new)
        return carry

    lax.fori_loop(0, width // 512, outer, 0)

    for t in range(1, NZ):
        for zo, ok, up in ((z - t, z - t >= 0, True), (z + t, z + t < NZ, False)):
            for xo in range(2):
                @pl.when(ok)
                def _(zo=zo, xo=xo):
                    arrived(wf.at[zo, xo, B], gb_r.at[zo, xo])
                if up:
                    gb_send(zo, xo, ok, False)
                else:
                    gb_send(zo, xo, False, ok)

        zt = NZ - 1 - t + z
        go = jnp.logical_and(jnp.logical_and(has_dn, zt < NZ), zt > z)

        @pl.when(go)
        def _(zt=zt, go=go):
            arrived(up_a.at[zt], sa_up.at[zt])
            add(into(part.at[zt, x, A]), [part.at[zt, x, A], xr_a.at[zt], up_a.at[zt]], rows_a)
            sa_send(zt, True, go)

        zd = t + z - (NZ - 1)
        gd = jnp.logical_and(jnp.logical_and(has_up, zd >= 0), zd < z)

        @pl.when(gd)
        def _(zd=zd, gd=gd):
            arrived(dn_a.at[zd], sa_dn.at[zd])
            add(into(part.at[zd, x, A]), [part.at[zd, x, A], xr_a.at[zd], dn_a.at[zd]], rows_a)
            sa_send(zd, False, gd)

        if t < NZ - 1:
            sa_start(t, True)
            sa_start(t, False)

        ready = {1: (), 2: (1, 2), 3: (3,)}[t]
        for zo, ok in ((z - t, z - t >= 0), (z + t, z + t < NZ)):
            @pl.when(ok)
            def _(zo=zo):
                use_b(zo, x)
        for k in ready:
            for zo, ok in ((z - k, z - k >= 0), (z + k, z + k < NZ)):
                @pl.when(ok)
                def _(zo=zo):
                    arrived(wf.at[zo, ox, A], gax_r.at[zo])
                    use(zo, ox, 0, rows)

    proj_ref[...] = acc[...].astype(BF16)

    arrived(xr_b, sbx.at[1])

    def last_b(i, carry):
        here = pl.ds(pl.multiple_of(i * 32, 32), 32)
        there = pl.ds(pl.multiple_of(rows_a + i * 32, 32), 32)
        wg_ref[there, :] = (wg_ref[there, :] + xr_b[here, :].astype(F32)) * scaling
        return carry

    lax.fori_loop(0, rows_b // 32, last_b, 0)

    def wg_a(here, total):
        wg_ref[here, :] = total * scaling

    own = [part.at[z, x, A], xr_a.at[z]]

    @pl.when(has_dn)
    def _():
        arrived(up_a.at[z], sa_up.at[z])

    @pl.when(has_up)
    def _():
        arrived(dn_a.at[z], sa_dn.at[z])

    @pl.when(jnp.logical_and(has_dn, has_up))
    def _():
        add(wg_a, own + [up_a.at[z], dn_a.at[z]], rows_a)

    @pl.when(jnp.logical_not(has_dn))
    def _():
        add(wg_a, own + [dn_a.at[z]], rows_a)

    @pl.when(jnp.logical_not(has_up))
    def _():
        add(wg_a, own + [up_a.at[z]], rows_a)

    for cond, early, copy in pending:
        if early is not None:
            cond = jnp.logical_and(cond, jnp.logical_not(early))
        if cond is None:
            copy().wait_send()
        else:
            pl.when(cond)(lambda copy=copy: copy().wait_send())


def grid_local(
    islands,
    tokens, cotangent, key_weight, quant_codes, zero_points, minima, quant_steps, momentum, params
):
    tok_rows, width = tokens.shape[1:]
    rows, heads = key_weight.shape[1:]
    frag, groups = zero_points.shape[1:]
    rows_a = rows * 3 // 5 // 32 * 32
    rows_b = rows - rows_a
    scaling = 1.0 / math.sqrt(tok_rows * 2 * NZ)
    vmem = pl.BlockSpec(memory_space=pltpu.VMEM)
    hbm = pl.BlockSpec(memory_space=pltpu.HBM)
    dma = pltpu.SemaphoreType.DMA
    outs = pl.pallas_call(
        functools.partial(kernel, islands, rows_a, scaling),
        out_shape=(
            pltpu.VMEM((tok_rows, heads), BF16),
            pltpu.VMEM((tok_rows, width), BF16),
            pltpu.VMEM((rows, heads), F32),
            pltpu.VMEM((frag, width), F32),
            pltpu.VMEM((frag, width), F32),
        ),
        in_specs=[hbm] * 9,
        out_specs=[vmem] * 5,
        scratch_shapes=[
            pltpu.VMEM((tok_rows, width), BF16),
            pltpu.VMEM((tok_rows, heads), BF16),
            pltpu.VMEM((frag, width), jnp.int32),
            pltpu.VMEM((frag, groups), jnp.int32),
            pltpu.VMEM((frag, groups), F32),
            pltpu.VMEM((frag, groups), F32),
            pltpu.VMEM((frag, width), F32),
            pltpu.VMEM((frag, width), F32),
            pltpu.VMEM((NZ, 2, rows, heads), BF16),
            pltpu.VMEM((NZ, 2, rows, heads), BF16),
            pltpu.VMEM((NZ, rows_a, heads), BF16),
            pltpu.VMEM((NZ, rows_a, heads), BF16),
            pltpu.VMEM((NZ, rows_a, heads), BF16),
            pltpu.VMEM((NZ, 2, rows_b, heads), BF16),
            pltpu.VMEM((NZ, 2, rows_b, heads), BF16),
            pltpu.VMEM((rows_b, heads), BF16),
            pltpu.VMEM((islands, frag, width), BF16),
            pltpu.VMEM((tok_rows, heads), F32),
            dma((9,)),
            dma((NZ,)), dma((NZ,)), dma((NZ,)), dma((NZ,)), dma((NZ,)), dma((2,)),
            dma((NZ, 2)), dma((NZ, 2)), dma((NZ, 2)),
            dma((NZ,)), dma((NZ,)), dma((NZ,)), dma((NZ,)), dma((NZ,)),
            dma((NZ, 2)), dma((NZ, 2)), dma((NZ, 2)), dma((2,)),
            dma((islands - 1,)), dma((islands,)),
        ],
        compiler_params=pltpu.CompilerParams(
            collective_id=0, has_side_effects=True, vmem_limit_bytes=54 * 2**20
        ),
        cost_estimate=pl.CostEstimate(
            flops=6 * tok_rows * width * heads, bytes_accessed=20 * 2**20, transcendentals=0
        ),
    )(
        tokens[0], cotangent[0], key_weight[0], quant_codes[0], zero_points[0], minima[0],
        quant_steps[0], momentum, params,
    )
    projected, token_grad, weight_grad, new_momentum, new_params = outs
    return (projected[None], token_grad[None], weight_grad[None], new_momentum, new_params)


def solution(mesh):
    placed = (P("island", "fsdp", None),) * 7 + (P("fsdp", None),) * 2
    if mesh.shape["fsdp"] == 2 * NZ:
        body = functools.partial(grid_local, mesh.shape["island"])
    else:
        body = local
    return jax.shard_map(
        body,
        mesh=mesh,
        in_specs=placed,
        out_specs=(P("island", "fsdp", None),) * 3 + (P("fsdp", None),) * 2,
        check_vma=False,
    )
```

```python
import functools
import math

import jax
import jax.numpy as jnp
from jax import lax
from jax.experimental import pallas as pl
from jax.experimental.pallas import tpu as pltpu
from jax.sharding import PartitionSpec as P

GROUP = 128
MESH = pl.DeviceIdType.MESH
F32 = jnp.float32
BF16 = jnp.bfloat16
NZ = 4


def dequantize(quant_codes, zero_points, minima, quant_steps):
    shape = quant_codes.shape
    grouped = quant_codes.reshape(shape[:-1] + (shape[-1] // GROUP, GROUP))
    offset = (grouped - zero_points[..., None]).astype(F32)
    values = quant_steps[..., None] * offset + minima[..., None]
    return values.reshape(shape)


def local(
    tokens, cotangent, key_weight, quant_codes, zero_points, minima, quant_steps, momentum, params
):
    inputs = tokens[0]
    cot_rows = cotangent[0]
    weight = key_weight[0]
    island_tok = inputs.shape[0] * lax.axis_size("fsdp")
    scaling = 1.0 / math.sqrt(island_tok)
    piece = lax.all_gather(weight, "fsdp", axis=0, tiled=True)
    projected = jnp.dot(inputs, piece, preferred_element_type=F32).astype(BF16)
    back_acc = lax.dot_general(
        cot_rows, piece, (((1,), (1,)), ((), ())), preferred_element_type=F32
    ).astype(BF16)
    grad = lax.psum_scatter(
        lax.dot_general(inputs, cot_rows, (((0,), (0,)), ((), ())), preferred_element_type=F32),
        "fsdp",
        scatter_dimension=0,
        tiled=True,
    )
    weight_grad = grad * scaling
    values = dequantize(quant_codes[0], zero_points[0], minima[0], quant_steps[0])
    replicas = lax.axis_size("island")
    summed = lax.psum(values.astype(BF16), "island").astype(F32)
    delta = summed / replicas
    new_momentum = 0.9 * momentum + delta
    new_params = params - 0.7 * (delta + 0.9 * new_momentum)
    return (projected[None], back_acc[None], weight_grad[None], new_momentum, new_params)


def kernel(
    islands, rows_a, scaling,
    tok_hbm, cot_hbm, w_hbm, codes_hbm, zp_hbm, min_hbm, step_hbm, mom_hbm, par_hbm,
    proj_ref, tg_ref, wg_ref, nmom_ref, npar_ref,
    tok, cot_ref, codes_ref, zp_ref, min_ref, step_ref, mom_ref, par_ref, wf, part, xr_a, up_a, dn_a, up_b, dn_b, xr_b, vals, acc,
    in_sem, ga_up, ga_dn, ga_r, gax_s, gax_r, gbx, gb_up, gb_dn, gb_r,
    sax_s, sax_r, sa_s, sa_up, sa_dn, sb_s, sb_up, sb_dn, sbx, val_s, val_r,
):
    me = lax.axis_index("fsdp")
    isl = lax.axis_index("island")
    z, x = me // 2, me % 2
    ox = 1 - x
    rows = w_hbm.shape[0]
    A = pl.ds(0, rows_a)
    B = pl.ds(rows_a, rows - rows_a)
    flip = {"fsdp": me + 1 - 2 * x}
    above = {"fsdp": me + 2}
    below = {"fsdp": me - 2}
    has_up = z < NZ - 1
    has_dn = z > 0

    pending = []

    def send(make, to, cond=None, early=None):
        def copy():
            src, dst, ssem, rsem = make()
            return pltpu.make_async_remote_copy(
                src_ref=src, dst_ref=dst, send_sem=ssem, recv_sem=rsem,
                device_id=to, device_id_type=MESH)
        if early is not True:
            pending.append((cond, early, copy))
        copy().start()

    def arrived(dst, rsem):
        pltpu.make_async_remote_copy(
            src_ref=dst, dst_ref=dst, send_sem=rsem, recv_sem=rsem,
            device_id=flip, device_id_type=MESH).wait_recv()

    tok_in = pltpu.make_async_copy(tok_hbm, tok, in_sem.at[0])
    w_in = pltpu.make_async_copy(w_hbm, wf.at[z, x], in_sem.at[1])
    cot_in = pltpu.make_async_copy(cot_hbm, cot_ref, in_sem.at[2])
    quant_in = [
        pltpu.make_async_copy(src, dst, in_sem.at[3 + i])
        for i, (src, dst) in enumerate((
            (codes_hbm, codes_ref), (zp_hbm, zp_ref), (min_hbm, min_ref), (step_hbm, step_ref),
            (mom_hbm, mom_ref), (par_hbm, par_ref)))
    ]
    w_in.start()
    cot_in.start()
    tok_in.start()
    for copy in quant_in:
        copy.start()

    barrier = pltpu.get_barrier_semaphore()
    pl.semaphore_signal(barrier, inc=1, device_id=flip, device_id_type=MESH)

    @pl.when(has_up)
    def _():
        pl.semaphore_signal(barrier, inc=1, device_id=above, device_id_type=MESH)

    @pl.when(has_dn)
    def _():
        pl.semaphore_signal(barrier, inc=1, device_id=below, device_id_type=MESH)

    for hop in range(1, islands):
        pl.semaphore_signal(
            barrier, inc=1, device_id={"island": (isl + hop) % islands}, device_id_type=MESH)
    pl.semaphore_wait(barrier, islands + has_up.astype(jnp.int32) + has_dn.astype(jnp.int32))

    first, last = z == 0, z == NZ - 1

    def ga_send(zo, up, dn, own=False):
        c_up = jnp.logical_and(has_up, up)
        c_dn = jnp.logical_and(has_dn, dn)

        @pl.when(c_up)
        def _():
            send(lambda: (wf.at[zo, x, A], wf.at[zo, x, A], ga_up.at[zo], ga_r.at[zo]), above, c_up,
                 first if own else None)

        @pl.when(c_dn)
        def _():
            send(lambda: (wf.at[zo, x, A], wf.at[zo, x, A], ga_dn.at[zo], ga_r.at[zo]), below, c_dn,
                 last if own else None)

    def gax_send(zo, cond):
        send(lambda: (wf.at[zo, x, A], wf.at[zo, x, A], gax_s.at[zo], gax_r.at[zo]), flip, cond)

    def gb_send(zo, xo, up, dn, own=False):
        c_up = jnp.logical_and(has_up, up)
        c_dn = jnp.logical_and(has_dn, dn)

        @pl.when(c_up)
        def _():
            send(lambda: (wf.at[zo, xo, B], wf.at[zo, xo, B], gb_up.at[zo, xo], gb_r.at[zo, xo]),
                 above, c_up, first if own else None)

        @pl.when(c_dn)
        def _():
            send(lambda: (wf.at[zo, xo, B], wf.at[zo, xo, B], gb_dn.at[zo, xo], gb_r.at[zo, xo]),
                 below, c_dn, last if own else None)

    w_in.wait()
    send(lambda: (wf.at[z, x, B], wf.at[z, x, B], gbx.at[0], gbx.at[1]), flip)
    ga_send(z, True, True, own=True)

    cot_in.wait()
    tok_in.wait()
    cot = cot_ref[...]

    def sb_send(zt, xo, up, cond, early=None):
        if up:
            send(lambda: (part.at[zt, xo, B], up_b.at[zt, xo], sb_s.at[zt, xo], sb_up.at[zt, xo]),
                 above, cond, early)
        else:
            send(lambda: (part.at[zt, xo, B], dn_b.at[zt, xo], sb_s.at[zt, xo], sb_dn.at[zt, xo]),
                 below, cond, early)

    def sent(make, to):
        src, dst, ssem, rsem = make()
        pltpu.make_async_remote_copy(
            src_ref=src, dst_ref=dst, send_sem=ssem, recv_sem=rsem,
            device_id=to, device_id_type=MESH).wait_send()

    def sb_start(t, up):
        end = 0 if up else NZ - 1
        zt = NZ - 1 - t if up else t
        c = z == end
        to = above if up else below

        @pl.when(c)
        def _():
            if t == 0:
                if up:
                    sent(lambda: (wf.at[z, x, A], wf.at[z, x, A], ga_up.at[z], ga_r.at[z]), to)
                else:
                    sent(lambda: (wf.at[z, x, A], wf.at[z, x, A], ga_dn.at[z], ga_r.at[z]), to)
            else:
                before = zt + 1 if up else zt - 1
                sent(lambda: (part.at[before, 0, B], up_b.at[before, 0], sb_s.at[before, 0],
                              sb_up.at[before, 0]), to)
            for xo in range(2):
                sb_send(zt, xo, up, c, True if xo == 0 and t < NZ - 2 else None)

    tile = 256
    tiles = rows // tile
    for zt in (NZ - 1, 0, 2, 1):
        def grad_tile(i, carry, zt=zt):
            xo, r = i // tiles, (i % tiles) * tile
            cols = pl.ds(pl.multiple_of((zt * 2 + xo) * rows + r, tile), tile)
            part[zt, xo, pl.ds(pl.multiple_of(r, tile), tile), :] = lax.dot_general(
                tok[:, cols], cot, (((0,), (0,)), ((), ())), preferred_element_type=F32
            ).astype(BF16)
            return carry

        lax.fori_loop(0, 2 * tiles, grad_tile, 0)
        send(lambda zt=zt: (part.at[zt, ox, A], xr_a.at[zt], sax_s.at[zt], sax_r.at[zt]), flip)

    sb_start(0, True)
    sb_start(0, False)

    def gather_a(t):
        for zo, ok, up in ((z - t, z - t >= 0, True), (z + t, z + t < NZ, False)):
            @pl.when(ok)
            def _(zo=zo):
                arrived(wf.at[zo, x, A], ga_r.at[zo])
            if up:
                ga_send(zo, ok, False)
            else:
                ga_send(zo, False, ok)

    gather_a(1)
    for copy in quant_in:
        copy.wait()

    for g in range(zp_ref.shape[1]):
        span = slice(g * GROUP, (g + 1) * GROUP)
        one = slice(g, g + 1)
        offset = (codes_ref[:, span] - zp_ref[:, one]).astype(F32)
        vals[isl, :, span] = (step_ref[:, one] * offset + min_ref[:, one]).astype(BF16)
    for hop in range(1, islands):
        send(lambda hop=hop: (vals.at[isl], vals.at[isl], val_s.at[hop - 1], val_r.at[isl]),
             {"island": (isl + hop) % islands})

    acc[...] = jnp.zeros_like(acc)

    def use(zo, xo, first, count):
        def body(i, carry):
            r = pl.multiple_of(first + i * 128, 128)
            cols = pl.ds(pl.multiple_of((zo * 2 + xo) * rows + r, 128), 128)
            block = wf[zo, xo, pl.ds(r, 128), :]
            acc[...] += jnp.dot(tok[:, cols], block, preferred_element_type=F32)
            tg_ref[:, cols] = lax.dot_general(
                cot_ref[...], block, (((1,), (1,)), ((), ())), preferred_element_type=F32
            ).astype(BF16)
            return carry

        lax.fori_loop(0, count // 128, body, 0)

    half = rows // 2

    def use_a(zo, xo):
        use(zo, xo, 0, half)

    def use_b(zo, xo):
        use(zo, xo, half, rows - half)

    def add(write, reads, count):
        def body(i, carry):
            here = pl.ds(pl.multiple_of(i * 32, 32), 32)
            total = reads[0][here, :].astype(F32)
            for ref in reads[1:]:
                total += ref[here, :].astype(F32)
            write(here, total)
            return carry

        lax.fori_loop(0, count // 32, body, 0)

    def into(ref):
        def write(here, total):
            ref[here, :] = total.astype(BF16)
        return write

    use(z, x, 0, rows)

    def gb_open():
        arrived(wf.at[z, ox, B], gbx.at[1])
        gb_send(z, x, z != NZ - 2, z != 1, own=True)
        gb_send(z, ox, True, True)

    rows_b = rows - rows_a

    gather_a(2)
    gb_send(z, x, z == NZ - 2, z == 1)
    for t in range(1, NZ - 1):
        zt = NZ - 1 - t + z
        c = jnp.logical_and(has_dn, zt < NZ)
        go = jnp.logical_and(c, zt > z)

        @pl.when(go)
        def _(zt=zt, go=go):
            for xo in range(2):
                arrived(up_b.at[zt, xo], sb_up.at[zt, xo])
                add(into(part.at[zt, xo, B]), [part.at[zt, xo, B], up_b.at[zt, xo]], rows_b)
                sb_send(zt, xo, True, go)

        zd = t + z - (NZ - 1)
        c = jnp.logical_and(has_up, zd >= 0)
        gd = jnp.logical_and(c, zd < z)

        @pl.when(gd)
        def _(zd=zd, gd=gd):
            for xo in range(2):
                arrived(dn_b.at[zd, xo], sb_dn.at[zd, xo])
                add(into(part.at[zd, xo, B]), [part.at[zd, xo, B], dn_b.at[zd, xo]], rows_b)
                sb_send(zd, xo, False, gd)

        sb_start(t, True)
        sb_start(t, False)
        if t == NZ - 2:
            gb_open()
            arrived(xr_a.at[NZ - 1], sax_r.at[NZ - 1])
            gax_send(z, None)
        for zo, ok in ((z - t, z - t >= 0), (z + t, z + t < NZ)):
            @pl.when(ok)
            def _(zo=zo):
                use_a(zo, x)

    gather_a(NZ - 1)

    def b_sums(xo, write):
        own = part.at[z, xo, B]

        @pl.when(has_dn)
        def _():
            arrived(up_b.at[z, xo], sb_up.at[z, xo])

        @pl.when(has_up)
        def _():
            arrived(dn_b.at[z, xo], sb_dn.at[z, xo])

        @pl.when(jnp.logical_and(has_dn, has_up))
        def _():
            add(write, [own, up_b.at[z, xo], dn_b.at[z, xo]], rows_b)

        @pl.when(jnp.logical_not(has_dn))
        def _():
            add(write, [own, dn_b.at[z, xo]], rows_b)

        @pl.when(jnp.logical_not(has_up))
        def _():
            add(write, [own, up_b.at[z, xo]], rows_b)

    for zo, ok in ((z - NZ + 1, z - NZ + 1 >= 0), (z + NZ - 1, z + NZ - 1 < NZ)):
        @pl.when(ok)
        def _(zo=zo):
            use_a(zo, x)

    def wg_b(here, total):
        wg_ref[pl.ds(pl.multiple_of(rows_a + here.start, 32), 32), :] = total

    def sa_send(zt, up, cond, early=None):
        if up:
            send(lambda: (part.at[zt, x, A], up_a.at[zt], sa_s.at[zt], sa_up.at[zt]), above, cond,
                 early)
        else:
            send(lambda: (part.at[zt, x, A], dn_a.at[zt], sa_s.at[zt], sa_dn.at[zt]), below, cond,
                 early)

    def sa_start(t, up):
        zt = NZ - 1 - t if up else t
        c = first if up else last
        to = above if up else below

        @pl.when(c)
        def _():
            add(into(part.at[zt, x, A]), [part.at[zt, x, A], xr_a.at[zt]], rows_a)
            if t == 0:
                if up:
                    sent(lambda: (wf.at[z, x, B], wf.at[z, x, B], gb_up.at[z, x], gb_r.at[z, x]), to)
                else:
                    sent(lambda: (wf.at[z, x, B], wf.at[z, x, B], gb_dn.at[z, x], gb_r.at[z, x]), to)
            else:
                before = zt + 1 if up else zt - 1
                sent(lambda: (part.at[before, x, A], up_a.at[before], sa_s.at[before],
                              sa_up.at[before]), to)
            sa_send(zt, up, c, True if t < NZ - 2 else None)

    for zt, t in ((0, 1), (2, 2), (1, 3)):
        arrived(xr_a.at[zt], sax_r.at[zt])
        for zo, ok in ((z - t, z - t >= 0), (z + t, z + t < NZ)):
            @pl.when(ok)
            def _(zo=zo, ok=ok):
                gax_send(zo, ok)
    sa_start(0, True)
    sa_start(0, False)

    b_sums(ox, into(part.at[z, ox, B]))
    send(lambda: (part.at[z, ox, B], xr_b, sbx.at[0], sbx.at[1]), flip)
    b_sums(x, wg_b)

    arrived(wf.at[z, ox, A], gax_r.at[z])
    use(z, ox, 0, rows)

    for hop in range(1, islands):
        other = (isl + hop) % islands
        arrived(vals.at[other], val_r.at[other])

    width = codes_ref.shape[1]

    def outer(i, carry):
        span = pl.ds(pl.multiple_of(i * 512, 512), 512)
        total = vals[0, :, span].astype(F32)
        for j in range(1, islands):
            total += vals[j, :, span].astype(F32)
        delta = total / islands
        new = 0.9 * mom_ref[:, span] + delta
        nmom_ref[:, span] = new
        npar_ref[:, span] = par_ref[:, span] - 0.7 * (delta + 0.9 * new)
        return carry

    lax.fori_loop(0, width // 512, outer, 0)

    for t in range(1, NZ):
        for zo, ok, up in ((z - t, z - t >= 0, True), (z + t, z + t < NZ, False)):
            for xo in range(2):
                @pl.when(ok)
                def _(zo=zo, xo=xo):
                    arrived(wf.at[zo, xo, B], gb_r.at[zo, xo])
                if up:
                    gb_send(zo, xo, ok, False)
                else:
                    gb_send(zo, xo, False, ok)

        zt = NZ - 1 - t + z
        go = jnp.logical_and(jnp.logical_and(has_dn, zt < NZ), zt > z)

        @pl.when(go)
        def _(zt=zt, go=go):
            arrived(up_a.at[zt], sa_up.at[zt])
            add(into(part.at[zt, x, A]), [part.at[zt, x, A], xr_a.at[zt], up_a.at[zt]], rows_a)
            sa_send(zt, True, go)

        zd = t + z - (NZ - 1)
        gd = jnp.logical_and(jnp.logical_and(has_up, zd >= 0), zd < z)

        @pl.when(gd)
        def _(zd=zd, gd=gd):
            arrived(dn_a.at[zd], sa_dn.at[zd])
            add(into(part.at[zd, x, A]), [part.at[zd, x, A], xr_a.at[zd], dn_a.at[zd]], rows_a)
            sa_send(zd, False, gd)

        if t < NZ - 1:
            sa_start(t, True)
            sa_start(t, False)

        ready = {1: (), 2: (1, 2), 3: (3,)}[t]
        for zo, ok in ((z - t, z - t >= 0), (z + t, z + t < NZ)):
            @pl.when(ok)
            def _(zo=zo):
                use_b(zo, x)
        for k in ready:
            for zo, ok in ((z - k, z - k >= 0), (z + k, z + k < NZ)):
                @pl.when(ok)
                def _(zo=zo):
                    arrived(wf.at[zo, ox, A], gax_r.at[zo])
                    use(zo, ox, 0, rows)

    proj_ref[...] = acc[...].astype(BF16)

    arrived(xr_b, sbx.at[1])

    def last_b(i, carry):
        here = pl.ds(pl.multiple_of(i * 32, 32), 32)
        there = pl.ds(pl.multiple_of(rows_a + i * 32, 32), 32)
        wg_ref[there, :] = (wg_ref[there, :] + xr_b[here, :].astype(F32)) * scaling
        return carry

    lax.fori_loop(0, rows_b // 32, last_b, 0)

    def wg_a(here, total):
        wg_ref[here, :] = total * scaling

    own = [part.at[z, x, A], xr_a.at[z]]

    @pl.when(has_dn)
    def _():
        arrived(up_a.at[z], sa_up.at[z])

    @pl.when(has_up)
    def _():
        arrived(dn_a.at[z], sa_dn.at[z])

    @pl.when(jnp.logical_and(has_dn, has_up))
    def _():
        add(wg_a, own + [up_a.at[z], dn_a.at[z]], rows_a)

    @pl.when(jnp.logical_not(has_dn))
    def _():
        add(wg_a, own + [dn_a.at[z]], rows_a)

    @pl.when(jnp.logical_not(has_up))
    def _():
        add(wg_a, own + [up_a.at[z]], rows_a)

    for cond, early, copy in pending:
        if early is not None:
            cond = jnp.logical_and(cond, jnp.logical_not(early))
        if cond is None:
            copy().wait_send()
        else:
            pl.when(cond)(lambda copy=copy: copy().wait_send())


def grid_local(
    islands,
    tokens, cotangent, key_weight, quant_codes, zero_points, minima, quant_steps, momentum, params
):
    tok_rows, width = tokens.shape[1:]
    rows, heads = key_weight.shape[1:]
    frag, groups = zero_points.shape[1:]
    rows_a = rows * 3 // 5 // 32 * 32
    rows_b = rows - rows_a
    scaling = 1.0 / math.sqrt(tok_rows * 2 * NZ)
    vmem = pl.BlockSpec(memory_space=pltpu.VMEM)
    hbm = pl.BlockSpec(memory_space=pltpu.HBM)
    dma = pltpu.SemaphoreType.DMA
    outs = pl.pallas_call(
        functools.partial(kernel, islands, rows_a, scaling),
        out_shape=(
            pltpu.VMEM((tok_rows, heads), BF16),
            pltpu.VMEM((tok_rows, width), BF16),
            pltpu.VMEM((rows, heads), F32),
            pltpu.VMEM((frag, width), F32),
            pltpu.VMEM((frag, width), F32),
        ),
        in_specs=[hbm] * 9,
        out_specs=[vmem] * 5,
        scratch_shapes=[
            pltpu.VMEM((tok_rows, width), BF16),
            pltpu.VMEM((tok_rows, heads), BF16),
            pltpu.VMEM((frag, width), jnp.int32),
            pltpu.VMEM((frag, groups), jnp.int32),
            pltpu.VMEM((frag, groups), F32),
            pltpu.VMEM((frag, groups), F32),
            pltpu.VMEM((frag, width), F32),
            pltpu.VMEM((frag, width), F32),
            pltpu.VMEM((NZ, 2, rows, heads), BF16),
            pltpu.VMEM((NZ, 2, rows, heads), BF16),
            pltpu.VMEM((NZ, rows_a, heads), BF16),
            pltpu.VMEM((NZ, rows_a, heads), BF16),
            pltpu.VMEM((NZ, rows_a, heads), BF16),
            pltpu.VMEM((NZ, 2, rows_b, heads), BF16),
            pltpu.VMEM((NZ, 2, rows_b, heads), BF16),
            pltpu.VMEM((rows_b, heads), BF16),
            pltpu.VMEM((islands, frag, width), BF16),
            pltpu.VMEM((tok_rows, heads), F32),
            dma((9,)),
            dma((NZ,)), dma((NZ,)), dma((NZ,)), dma((NZ,)), dma((NZ,)), dma((2,)),
            dma((NZ, 2)), dma((NZ, 2)), dma((NZ, 2)),
            dma((NZ,)), dma((NZ,)), dma((NZ,)), dma((NZ,)), dma((NZ,)),
            dma((NZ, 2)), dma((NZ, 2)), dma((NZ, 2)), dma((2,)),
            dma((islands - 1,)), dma((islands,)),
        ],
        compiler_params=pltpu.CompilerParams(
            collective_id=0, has_side_effects=True, vmem_limit_bytes=54 * 2**20
        ),
        cost_estimate=pl.CostEstimate(
            flops=6 * tok_rows * width * heads, bytes_accessed=20 * 2**20, transcendentals=0
        ),
    )(
        tokens[0], cotangent[0], key_weight[0], quant_codes[0], zero_points[0], minima[0],
        quant_steps[0], momentum, params,
    )
    projected, token_grad, weight_grad, new_momentum, new_params = outs
    return (projected[None], token_grad[None], weight_grad[None], new_momentum, new_params)


def solution(mesh):
    placed = (P("island", "fsdp", None),) * 7 + (P("fsdp", None),) * 2
    if mesh.shape["fsdp"] == 2 * NZ:
        body = functools.partial(grid_local, mesh.shape["island"])
    else:
        body = local
    return jax.shard_map(
        body,
        mesh=mesh,
        in_specs=placed,
        out_specs=(P("island", "fsdp", None),) * 3 + (P("fsdp", None),) * 2,
        check_vma=False,
    )
```
